32 devices in a mesh: row: 16 (over z, x, core), col: 2 (over y).
Axes of the slice: x: 2, y: 2, z: 4, core: 2. Of those that a mesh axis runs over, the one named last changes fastest.
Arguments:
- features: bfloat16 [128, 32768], P(None, 'row'), may hold values from -6 to 6
- weight_in: bfloat16 [128, 512], P(None, 'col'), may hold values from -0.5 to 0.5
- weight_out: bfloat16 [512, 64], replicated, may hold values from -0.25 to 0.25
- score_grad: bfloat16 [64, 32768], P('col', 'row'), may hold values from -0.011962891 to 0.011962891
- band_blocks: bfloat16 [256, 3, 128, 128], P('row'), may hold values from -0.25 to 0.25
- long_blocks: bfloat16 [192, 128, 128], P('row'), may hold values from -0.25 to 0.25
- long_rows: int32 [16, 12], P('row'), may hold values from 0 to 15
- long_sources: int32 [16, 12], replicated, may hold values from 0 to 255, as said below
- long_counts: int32 [16], replicated, may hold values from 1 to 12, as said below
Outputs:
- scores: bfloat16 [64, 32768], P('col', 'row')
- first_grad: float32 [128, 512], P(None, 'col')
- second_grad: float32 [512, 64], P('col')
The draws below stay inside these ranges and needn't reach their ends.
Inputs may be any that keep to these rules, and one draw needn't show every extreme that they name: `long_sources`: every slot's block column lies on a partition at cycle distance 1 to 3 from the slot's own partition (either direction, indices taken mod the number of partitions); over ALL 12 slots of a partition each of the 6 such partitions is read by exactly 2 slots. Slots s < long_counts[p] are live, the others are ignored; some partition has all 12 live.
All inputs are finite; a program needn't handle non-finite values.
Results may differ from the reference program's by a relative error of at most 0.0065.
Values may be sent and summed in bfloat16 or wider, within the bound.
A program may use at most 128 MiB of HBM per device.

```python
import jax
import jax.numpy as jnp

BLK = 128
NB = 16
REACH = 3
CAP = 2
SLOTS = 12
F_IN = 128
H = 512
C = 64
BLOCKS = 256
NODES = 32768
LONG_ALL = 192
N_ROW = 16


def draw_long_sources(key, part):
    key_order = jax.random.fold_in(key, 11)
    key_local = jax.random.fold_in(key, 12)
    offset_list = jnp.repeat(jnp.array([distance for distance in range(-REACH, REACH + 1) if distance != 0], jnp.int32), CAP)
    scores_int = jax.random.randint(key_order, (N_ROW, SLOTS), 0, 1 << 20) * SLOTS + jnp.arange(SLOTS, dtype=jnp.int32)[None, :]
    shuffle = jnp.argsort(scores_int, axis=1)
    offsets = offset_list[shuffle]
    partition = jnp.arange(N_ROW, dtype=jnp.int32)[:, None]
    owners = jnp.mod(partition + offsets, N_ROW)
    local_blocks = jax.random.randint(key_local, (N_ROW, SLOTS), 0, NB)
    return (owners * NB + local_blocks).astype(jnp.int32)


def draw_long_counts(key, part):
    first_draw = jax.random.randint(jax.random.fold_in(key, 21), (N_ROW,), 0, SLOTS + 1)
    second_draw = jax.random.randint(jax.random.fold_in(key, 22), (N_ROW,), 0, SLOTS + 1)
    counts_drawn = 1 + first_draw * second_draw // (SLOTS + 1)
    fullest = jax.random.randint(jax.random.fold_in(key, 23), (), 0, N_ROW)
    return jnp.where(jnp.arange(N_ROW, dtype=jnp.int32) == fullest, SLOTS, counts_drawn).astype(jnp.int32)


def plant(values, key, low, largest):
    longest = values.shape.index(max(values.shape))
    spots = []
    for shift in (0, 1):
        where = [jax.random.randint(jax.random.fold_in(key, axis), (), 0, length) for axis, length in enumerate(values.shape)]
        where[longest] = (where[longest] + shift) % values.shape[longest]
        spots.append(tuple(where))
    return values.at[spots[0]].set(low).at[spots[1]].set(largest)


def block_levels(stream_key, extent, pieces, least, largest):
    def one(dim, blocks):
        heights = jax.random.uniform(jax.random.fold_in(jax.random.fold_in(stream_key, 6), dim), (blocks,), jnp.float32, least / len(pieces), largest / len(pieces))
        return jnp.repeat(jnp.exp(heights), extent[dim] // blocks).reshape((-1,) + (1,) * (len(extent) - dim - 1))

    level = one(*pieces[0])
    for cut in pieces[1:]:
        level = level * one(*cut)
    return level


def noise(key, shape, width, bound, pieces=(), kind=jnp.bfloat16):
    drawn = jax.random.normal(key, shape, jnp.float32) * width
    if len(pieces) > 0:
        drawn = block_levels(key, shape, pieces, -0.22, 0.18) * drawn
    return jnp.clip(drawn, min=-bound, max=bound).astype(kind)


def setup_inputs(seed: int = 0) -> dict:
    seeds = jax.random.split(jax.random.key(seed), 10)
    features = noise(seeds[0], (F_IN, NODES), 1.0, 6.0, ((1, 16),))
    weight_in = noise(seeds[1], (F_IN, H), F_IN ** -0.5, 0.5, ((1, 2),))
    weight_out = noise(seeds[2], (H, C), H ** -0.5, 0.25)
    score_grad = noise(seeds[3], (C, NODES), 0.002, 0.011962891, ((0, 2), (1, 16)))
    band_blocks = noise(seeds[4], (BLOCKS, 3, BLK, BLK), (4 * BLK) ** -0.5, 0.25, ((0, 16),))
    long_blocks = noise(seeds[5], (LONG_ALL, BLK, BLK), (4 * BLK) ** -0.5, 0.25, ((0, 16),))
    long_rows = plant(jax.random.randint(seeds[6], (N_ROW, SLOTS), 0, NB), jax.random.fold_in(seeds[6], 1), 0, NB - 1).astype(jnp.int32)
    long_sources = draw_long_sources(jax.random.fold_in(seeds[9], 71), 0)
    long_counts = draw_long_counts(jax.random.fold_in(seeds[9], 71), 0)
    return {"features": features, "weight_in": weight_in, "weight_out": weight_out, "score_grad": score_grad, "band_blocks": band_blocks, "long_blocks": long_blocks, "long_rows": long_rows, "long_sources": long_sources, "long_counts": long_counts}


def slot_lists(long_rows, long_sources, long_counts):
    slot_order = jnp.arange(SLOTS, dtype=jnp.int32)
    is_live = (slot_order[None, :] < long_counts[:, None]).reshape(-1)
    targets = (jnp.arange(N_ROW, dtype=jnp.int32)[:, None] * NB + long_rows).reshape(-1).astype(jnp.int32)
    sources = long_sources.reshape(-1).astype(jnp.int32)
    return is_live, targets, sources


def band_product(values, band_blocks):
    rows_count = values.shape[0]
    blocks = values.reshape(rows_count, BLOCKS, BLK).astype(jnp.float32)
    band_wide = band_blocks.astype(jnp.float32)
    earlier = jnp.roll(blocks, 1, axis=1)
    onward = jnp.roll(blocks, -1, axis=1)
    summed = jnp.einsum('fgm,gnm->fgn', earlier, band_wide[:, 0])
    summed = summed + jnp.einsum('fgm,gnm->fgn', blocks, band_wide[:, 1])
    summed = summed + jnp.einsum('fgm,gnm->fgn', onward, band_wide[:, 2])
    return summed.reshape(rows_count, NODES)


def band_transpose(values, band_blocks):
    rows_count = values.shape[0]
    blocks = values.reshape(rows_count, BLOCKS, BLK).astype(jnp.float32)
    band_wide = band_blocks.astype(jnp.float32)
    to_prior = jnp.einsum('fgn,gnm->fgm', blocks, band_wide[:, 0])
    middle = jnp.einsum('fgn,gnm->fgm', blocks, band_wide[:, 1])
    to_later = jnp.einsum('fgn,gnm->fgm', blocks, band_wide[:, 2])
    summed = middle + jnp.roll(to_prior, -1, axis=1) + jnp.roll(to_later, 1, axis=1)
    return summed.reshape(rows_count, NODES)


def long_product(values, long_blocks, is_live, targets, sources):
    rows_count = values.shape[0]
    blocks = values.reshape(rows_count, BLOCKS, BLK).astype(jnp.float32)
    panels = jnp.take(blocks, sources, axis=1)
    contrib = jnp.einsum('fkm,knm->fkn', panels, long_blocks.astype(jnp.float32))
    contrib = contrib * is_live.astype(jnp.float32)[None, :, None]
    summed = jnp.zeros((rows_count, BLOCKS, BLK), jnp.float32).at[:, targets].add(contrib)
    return summed.reshape(rows_count, NODES)


def long_transpose(values, long_blocks, is_live, targets, sources):
    rows_count = values.shape[0]
    blocks = values.reshape(rows_count, BLOCKS, BLK).astype(jnp.float32)
    panels = jnp.take(blocks, targets, axis=1)
    contrib = jnp.einsum('fkn,knm->fkm', panels, long_blocks.astype(jnp.float32))
    contrib = contrib * is_live.astype(jnp.float32)[None, :, None]
    summed = jnp.zeros((rows_count, BLOCKS, BLK), jnp.float32).at[:, sources].add(contrib)
    return summed.reshape(rows_count, NODES)


def reference(features, weight_in, weight_out, score_grad, band_blocks, long_blocks, long_rows, long_sources, long_counts):
    is_live, targets, sources = slot_lists(long_rows, long_sources, long_counts)

    def aggregate(values):
        return band_product(values, band_blocks) + long_product(values, long_blocks, is_live, targets, sources)

    def aggregate_back(values):
        return band_transpose(values, band_blocks) + long_transpose(values, long_blocks, is_live, targets, sources)

    hidden_in = jnp.dot(weight_in.T, features, preferred_element_type=jnp.float32).astype(jnp.bfloat16)
    hidden_sum = aggregate(hidden_in)
    hidden_act = jax.nn.silu(hidden_sum).astype(jnp.bfloat16)
    class_in = jnp.dot(weight_out.T, hidden_act, preferred_element_type=jnp.float32).astype(jnp.bfloat16)
    scores = aggregate(class_in).astype(jnp.bfloat16)
    class_back = aggregate_back(score_grad).astype(jnp.bfloat16)
    second_grad = jnp.dot(hidden_act, class_back.T, preferred_element_type=jnp.float32)
    hidden_back = jnp.dot(weight_out, class_back, preferred_element_type=jnp.float32)
    sigmoid_val = jax.nn.sigmoid(hidden_sum)
    slope_back = (hidden_back * sigmoid_val * (1.0 + hidden_sum * (1.0 - sigmoid_val))).astype(jnp.bfloat16)
    input_back = aggregate_back(slope_back).astype(jnp.bfloat16)
    first_grad = jnp.dot(features, input_back.T, preferred_element_type=jnp.float32)
    return scores, first_grad, second_grad
```

```python
import functools

import jax
import jax.numpy as jnp
from jax import lax
from jax.experimental import pallas as pl
from jax.experimental.pallas import tpu as pltpu
from jax.sharding import PartitionSpec as P

BLK = 128
SLOTS = 12
DISTANCES = (-3, -2, -1, 1, 2, 3)
BEFORE = DISTANCES.index(-1)
BEYOND = DISTANCES.index(1)
MESH = pl.DeviceIdType.MESH
F32 = jnp.float32
BF16 = jnp.bfloat16


def nn(a, b):
    return lax.dot_general(a, b, (((1,), (0,)), ((), ())), preferred_element_type=F32)


def nt(a, b):
    return lax.dot_general(a, b, (((1,), (1,)), ((), ())), preferred_element_type=F32)


def lanes(block):
    if isinstance(block, int):
        return pl.ds(block * BLK, BLK)
    return pl.ds(pl.multiple_of(block * BLK, BLK), BLK)


def blocks_sent(pos):
    return 3 if pos in (BEFORE, BEYOND) else 2


def kernel(
    rows_n, cols_n, reduce_here,
    x_ref, win_ref, wout_ref, sg_ref, band_ref, long_ref, rows_ref, src_ref, count_ref,
    scores_ref, first_ref, second_ref,
    xb, sb, xs, xr, gs, gr, cs, cr, zacc, contrib, z, gacc, g2, slope, act, part, part_in, cls, red, red_in, summed,
    x_ss, x_rs, g_ss, g_rs, c_ss, c_rs, gc_ss, gc_rs, p_ss, p_rs, red_ss, red_rs, all_ss, all_rs,
):
    me = lax.axis_index("row")
    mc = lax.axis_index("col")
    nodes = x_ref.shape[1]
    nb = nodes // BLK
    hidden = win_ref.shape[1]
    cc = sg_ref.shape[0]
    wire = gs.dtype

    def row_at(by):
        return lax.rem(me + (by + rows_n), rows_n)

    def col_at(by):
        return lax.rem(mc + by, cols_n)

    barrier = pltpu.get_barrier_semaphore()
    if reduce_here:
        def greet(k, carry):
            pl.semaphore_signal(barrier, inc=1, device_id={"row": row_at(k)}, device_id_type=MESH)
            return carry
        lax.fori_loop(1, rows_n, greet, 0)
        expected = rows_n - 1
    else:
        for d in DISTANCES:
            pl.semaphore_signal(barrier, inc=1, device_id={"row": row_at(d)}, device_id_type=MESH)
        expected = len(DISTANCES)
    for k in range(1, cols_n):
        pl.semaphore_signal(barrier, inc=1, device_id={"col": col_at(k)}, device_id_type=MESH)
    expected += cols_n - 1

    def slots_of(reader, owner):
        low, high = jnp.int32(0), jnp.int32(0)
        for s in range(SLOTS):
            match = (lax.div(src_ref[reader, s], nb) == owner).astype(jnp.int32)
            high = jnp.maximum(high, match * s)
            low = jnp.maximum(low, match * (SLOTS - 1 - s))
        low = SLOTS - 1 - low
        return low, high

    served, read = [], []
    for d in DISTANCES:
        reader = row_at(-d)
        served.append([
            jnp.clip(src_ref[reader, s] - me * nb, 0, nb - 1) for s in slots_of(reader, me)
        ])
        read.append([
            (s, jnp.clip(rows_ref[0, s], 0, nb - 1), (s < count_ref[me]).astype(F32))
            for s in slots_of(me, row_at(d))
        ])

    for r in range(nb):
        xb[r] = x_ref[:, lanes(r)]
        sb[r] = sg_ref[:, lanes(r)].astype(wire)
    for pos in range(6):
        for rank in range(2):
            xs[pos, rank] = xb[served[pos][rank]]
    xs[BEFORE, 2] = xb[nb - 1]
    xs[BEYOND, 2] = xb[0]

    pl.semaphore_wait(barrier, expected)

    def swap(src, dst, ss, rs, pos, to):
        span = pl.ds(0, blocks_sent(pos))
        return pltpu.make_async_remote_copy(
            src_ref=src.at[pos, span], dst_ref=dst.at[pos, span],
            send_sem=ss.at[pos], recv_sem=rs.at[pos],
            device_id={"row": to}, device_id_type=MESH,
        )

    x_copies = [swap(xs, xr, x_ss, x_rs, pos, row_at(-d)) for pos, d in enumerate(DISTANCES)]
    for copy in x_copies:
        copy.start()

    for pos in range(6):
        for rank in range(2):
            s, row, live = read[pos][rank]
            out = nn(sb[row].astype(BF16), long_ref[s])
            gs[pos, rank] = (live * out).astype(wire)
    gs[BEFORE, 2] = nn(sg_ref[:, lanes(0)], band_ref[0, 0]).astype(wire)
    gs[BEYOND, 2] = nn(sg_ref[:, lanes(nb - 1)], band_ref[nb - 1, 2]).astype(wire)
    g_copies = [swap(gs, gr, g_ss, g_rs, pos, row_at(d)) for pos, d in enumerate(DISTANCES)]
    for copy in g_copies:
        copy.start()

    def g_band(r, first, last):
        total = nn(sg_ref[:, lanes(r)], band_ref[r, 1])
        if not last:
            total += nn(sg_ref[:, lanes(r + 1)], band_ref[r + 1, 0])
        if not first:
            total += nn(sg_ref[:, lanes(r - 1)], band_ref[r - 1, 2])
        gacc[r] = total

    def z_band(r, first, last):
        total = nt(x_ref[:, lanes(r)], band_ref[r, 1])
        if not first:
            total += nt(x_ref[:, lanes(r - 1)], band_ref[r, 0])
        if not last:
            total += nt(x_ref[:, lanes(r + 1)], band_ref[r, 2])
        zacc[r] = total

    def both(body):
        body(0, True, False)
        lax.fori_loop(1, nb - 1, lambda r, c: (body(r, False, False), c)[1], 0, unroll=2)
        body(nb - 1, False, True)

    both(g_band)

    for copy in g_copies:
        copy.wait_recv()
    gacc[0] += gr[BEYOND, 2].astype(F32)
    gacc[nb - 1] += gr[BEFORE, 2].astype(F32)

    def g_long(r, carry):
        total = gacc[r]
        for pos in range(6):
            for rank in range(2):
                total += (served[pos][rank] == r).astype(F32) * gr[pos, rank].astype(F32)
        g2[mc, :, lanes(r)] = total.astype(BF16).astype(wire)
        return carry

    lax.fori_loop(0, nb, g_long, 0)

    def g_share(k):
        return pltpu.make_async_remote_copy(
            src_ref=g2.at[mc], dst_ref=g2.at[mc],
            send_sem=gc_ss.at[k - 1], recv_sem=gc_rs.at[k - 1],
            device_id={"col": col_at(k)}, device_id_type=MESH,
        )

    def g_arrives(k):
        return pltpu.make_async_remote_copy(
            src_ref=g2.at[mc], dst_ref=g2.at[col_at(cols_n - k)],
            send_sem=gc_ss.at[k - 1], recv_sem=gc_rs.at[k - 1],
            device_id={"col": col_at(k)}, device_id_type=MESH,
        )

    g_shares = [g_share(k) for k in range(1, cols_n)]
    for copy in g_shares:
        copy.start()

    both(z_band)

    for copy in x_copies:
        copy.wait_recv()
    for pos in range(6):
        for rank in range(2):
            s, row, live = read[pos][rank]
            contrib[2 * pos + rank] = nt(xr[pos, rank], long_ref[s])
    zacc[0] += nt(xr[BEFORE, 2], band_ref[0, 0])
    zacc[nb - 1] += nt(xr[BEYOND, 2], band_ref[nb - 1, 2])

    def z_long(r, carry):
        total = zacc[r]
        for pos in range(6):
            for rank in range(2):
                s, row, live = read[pos][rank]
                total += (live * (row == r).astype(F32)) * contrib[2 * pos + rank]
        z[:, lanes(r)] = total.astype(BF16)
        return carry

    lax.fori_loop(0, nb, z_long, 0)

    win_t = win_ref[...].astype(F32).T.astype(BF16)
    my_out = wout_ref[pl.ds(pl.multiple_of(mc * hidden, hidden), hidden), :]
    out_t = my_out.astype(F32).T.astype(BF16)
    tile = 4 * BLK

    def tile_at(t):
        return pl.ds(pl.multiple_of(t * tile, tile), tile)

    def hidden_tile(t, carry):
        v = nn(win_t, z[:, tile_at(t)])
        sig = 0.5 * jnp.tanh(0.5 * v) + 0.5
        h = (v * sig).astype(BF16)
        act[:, tile_at(t)] = h
        slope[:, tile_at(t)] = sig * (1.0 + v * (1.0 - sig))
        p = nn(out_t, h)
        for c in range(cols_n):
            part[c, :, tile_at(t)] = p[c * cc:(c + 1) * cc]
        return carry

    lax.fori_loop(0, nodes // tile, hidden_tile, 0)

    def p_share(k):
        return pltpu.make_async_remote_copy(
            src_ref=part.at[col_at(k)], dst_ref=part_in.at[k - 1],
            send_sem=p_ss.at[k - 1], recv_sem=p_rs.at[k - 1],
            device_id={"col": col_at(k)}, device_id_type=MESH,
        )

    p_shares = [p_share(k) for k in range(1, cols_n)]
    for copy in p_shares:
        copy.start()

    for k in range(1, cols_n):
        g_arrives(k).wait_recv()

    first_ref[...] = jnp.zeros_like(first_ref)
    second_ref[...] = jnp.zeros_like(second_ref)

    def grad_tile(t, carry):
        g = g2[:, :, tile_at(t)].reshape(cols_n * cc, tile).astype(BF16)
        h = act[:, tile_at(t)]
        second_ref[...] += nt(g, h)
        ds = (nn(my_out, g) * slope[:, tile_at(t)]).astype(BF16)
        first_ref[...] += nt(z[:, tile_at(t)], ds)
        return carry

    lax.fori_loop(0, nodes // tile, grad_tile, 0)

    if reduce_here:
        fr = first_ref.shape[0] // rows_n
        sr = second_ref.shape[0] // rows_n
        for j in range(rows_n):
            red[j, 0:fr] = first_ref[j * fr:(j + 1) * fr]
            red[j, fr:fr + sr] = second_ref[j * sr:(j + 1) * sr]

        def red_copy(k):
            return pltpu.make_async_remote_copy(
                src_ref=red.at[row_at(k)], dst_ref=red_in.at[k - 1],
                send_sem=red_ss.at[k - 1], recv_sem=red_rs.at[k - 1],
                device_id={"row": row_at(k)}, device_id_type=MESH,
            )

        def all_copy(k, slot):
            return pltpu.make_async_remote_copy(
                src_ref=summed.at[me], dst_ref=summed.at[slot],
                send_sem=all_ss.at[k - 1], recv_sem=all_rs.at[k - 1],
                device_id={"row": row_at(k)}, device_id_type=MESH,
            )

        def over_peers(body):
            lax.fori_loop(1, rows_n, lambda k, c: (body(k), c)[1], 0)

        over_peers(lambda k: red_copy(k).start())

    for copy in p_shares:
        copy.wait_recv()

    def class_block(r, carry):
        total = part[mc, :, lanes(r)]
        for k in range(cols_n - 1):
            total += part_in[k, :, lanes(r)]
        cls[r] = total.astype(BF16).astype(wire)
        return carry

    lax.fori_loop(0, nb, class_block, 0, unroll=4)

    for pos in range(6):
        for rank in range(2):
            cs[pos, rank] = cls[served[pos][rank]]
    cs[BEFORE, 2] = cls[nb - 1]
    cs[BEYOND, 2] = cls[0]
    c_copies = [swap(cs, cr, c_ss, c_rs, pos, row_at(-d)) for pos, d in enumerate(DISTANCES)]
    for copy in c_copies:
        copy.start()

    def s_band(r, first, last):
        total = nt(cls[r].astype(BF16), band_ref[r, 1])
        if not first:
            total += nt(cls[r - 1].astype(BF16), band_ref[r, 0])
        if not last:
            total += nt(cls[r + 1].astype(BF16), band_ref[r, 2])
        gacc[r] = total

    both(s_band)

    if reduce_here:
        over_peers(lambda k: red_copy(k).wait_recv())
        total = red[me]
        for k in range(rows_n - 1):
            total += red_in[k]
        summed[me] = total
        over_peers(lambda k: all_copy(k, me).start())

    for copy in c_copies:
        copy.wait_recv()
    for pos in range(6):
        for rank in range(2):
            s, row, live = read[pos][rank]
            contrib[2 * pos + rank, 0:cc] = nt(cr[pos, rank].astype(BF16), long_ref[s])
    gacc[0] += nt(cr[BEFORE, 2].astype(BF16), band_ref[0, 0])
    gacc[nb - 1] += nt(cr[BEYOND, 2].astype(BF16), band_ref[nb - 1, 2])

    def s_long(r, carry):
        total = gacc[r]
        for pos in range(6):
            for rank in range(2):
                s, row, live = read[pos][rank]
                total += (live * (row == r).astype(F32)) * contrib[2 * pos + rank, 0:cc]
        scores_ref[:, lanes(r)] = total.astype(BF16)
        return carry

    lax.fori_loop(0, nb, s_long, 0)

    if reduce_here:
        over_peers(lambda k: all_copy(k, row_at(-k)).wait_recv())
        for j in range(rows_n):
            first_ref[j * fr:(j + 1) * fr] = summed[j, 0:fr]
            second_ref[j * sr:(j + 1) * sr] = summed[j, fr:fr + sr]
        over_peers(lambda k: red_copy(k).wait_send())
        over_peers(lambda k: all_copy(k, me).wait_send())

    for copy in x_copies + g_copies + c_copies + g_shares + p_shares:
        copy.wait_send()


def local(
    features, weight_in, weight_out, score_grad, band_blocks, long_blocks, long_rows, long_sources, long_counts,
):
    rows_n = lax.axis_size("row")
    cols_n = lax.axis_size("col")
    feats, nodes = features.shape
    nb = nodes // BLK
    hidden = weight_in.shape[1]
    cc = score_grad.shape[0]
    classes = weight_out.shape[1]
    wire = BF16 if cc % 16 == 0 else F32
    reduce_here = feats % (8 * rows_n) == 0 and classes % rows_n == 0 and hidden % BLK == 0
    chunk = (feats + classes) // rows_n if reduce_here else 8
    slices = rows_n if reduce_here else 1
    peers = max(slices - 1, 1)
    dma = pltpu.SemaphoreType.DMA
    vmem = pl.BlockSpec(memory_space=pltpu.VMEM)
    smem = pl.BlockSpec(memory_space=pltpu.SMEM)
    scores, first, second = pl.pallas_call(
        functools.partial(kernel, rows_n, cols_n, reduce_here),
        out_shape=(
            jax.ShapeDtypeStruct((cc, nodes), BF16),
            jax.ShapeDtypeStruct((feats, hidden), F32),
            jax.ShapeDtypeStruct((classes, hidden), F32),
        ),
        in_specs=[vmem] * 6 + [smem] * 3,
        out_specs=(vmem, vmem, vmem),
        scratch_shapes=[
            pltpu.VMEM((nb, feats, BLK), BF16),
            pltpu.VMEM((nb, cc, BLK), wire),
            pltpu.VMEM((6, 3, feats, BLK), BF16),
            pltpu.VMEM((6, 3, feats, BLK), BF16),
            pltpu.VMEM((6, 3, cc, BLK), wire),
            pltpu.VMEM((6, 3, cc, BLK), wire),
            pltpu.VMEM((6, 3, cc, BLK), wire),
            pltpu.VMEM((6, 3, cc, BLK), wire),
            pltpu.VMEM((nb, feats, BLK), F32),
            pltpu.VMEM((SLOTS, feats, BLK), F32),
            pltpu.VMEM((feats, nodes), BF16),
            pltpu.VMEM((nb, cc, BLK), F32),
            pltpu.VMEM((cols_n, cc, nodes), wire),
            pltpu.VMEM((hidden, nodes), F32),
            pltpu.VMEM((hidden, nodes), BF16),
            pltpu.VMEM((cols_n, cc, nodes), F32),
            pltpu.VMEM((cols_n - 1, cc, nodes), F32),
            pltpu.VMEM((nb, cc, BLK), wire),
            pltpu.VMEM((slices, chunk, hidden), F32),
            pltpu.VMEM((peers, chunk, hidden), F32),
            pltpu.VMEM((slices, chunk, hidden), F32),
            dma((6,)), dma((6,)), dma((6,)), dma((6,)), dma((6,)), dma((6,)),
            dma((cols_n - 1,)), dma((cols_n - 1,)), dma((cols_n - 1,)), dma((cols_n - 1,)),
            dma((peers,)), dma((peers,)), dma((peers,)), dma((peers,)),
        ],
        compiler_params=pltpu.CompilerParams(
            collective_id=0, has_side_effects=True, vmem_limit_bytes=40 * 1024 * 1024
        ),
    )(features, weight_in, weight_out, score_grad, band_blocks, long_blocks, long_rows, long_sources, long_counts)
    second = second.T
    if not reduce_here:
        first, second = lax.psum((first, second), "row")
    return scores, first, second


def solution(mesh):
    return jax.shard_map(
        local,
        mesh=mesh,
        in_specs=(
            P(None, "row"),
            P(None, "col"),
            P(),
            P("col", "row"),
            P("row", None, None, None),
            P("row", None, None),
            P("row", None),
            P(),
            P(),
        ),
        out_specs=(P("col", "row"), P(None, "col"), P("col", None)),
        check_vma=False,
    )
```

```python
import functools

import jax
import jax.numpy as jnp
from jax import lax
from jax.experimental import pallas as pl
from jax.experimental.pallas import tpu as pltpu
from jax.sharding import PartitionSpec as P

BLK = 128
SLOTS = 12
DISTANCES = (-3, -2, -1, 1, 2, 3)
BEFORE = DISTANCES.index(-1)
BEYOND = DISTANCES.index(1)
MESH = pl.DeviceIdType.MESH
F32 = jnp.float32
BF16 = jnp.bfloat16


def nn(a, b):
    return lax.dot_general(a, b, (((1,), (0,)), ((), ())), preferred_element_type=F32)


def nt(a, b):
    return lax.dot_general(a, b, (((1,), (1,)), ((), ())), preferred_element_type=F32)


def lanes(block):
    if isinstance(block, int):
        return pl.ds(block * BLK, BLK)
    return pl.ds(pl.multiple_of(block * BLK, BLK), BLK)


def blocks_sent(pos):
    return 3 if pos in (BEFORE, BEYOND) else 2


def kernel(
    rows_n, cols_n, reduce_here,
    x_hbm, win_hbm, wout_hbm, sg_hbm, band_hbm, long_hbm, rows_hbm, src_hbm, count_hbm,
    scores_ref, first_ref, second_ref,
    x_ref, win_ref, wout_ref, sg_ref, band_ref, long_ref, rows_ref, src_ref, count_ref, in_sem,
    xb, sb, xs, xr, gs, gr, cs, cr, zacc, contrib, z, gacc, g2, part, part_out, part_in, cls, red, red_in, summed,
    x_ss, x_rs, g_ss, g_rs, c_ss, c_rs, gc_ss, gc_rs, p_ss, p_rs, red_ss, red_rs, all_ss, all_rs,
):
    me = lax.axis_index("row")
    mc = lax.axis_index("col")
    nodes = x_ref.shape[1]
    nb = nodes // BLK
    hidden = win_ref.shape[1]
    cc = sg_ref.shape[0]
    wire = gs.dtype

    operands = [
        pltpu.make_async_copy(src, dst, in_sem.at[i])
        for i, (src, dst) in enumerate((
            (rows_hbm, rows_ref), (src_hbm, src_ref), (count_hbm, count_ref), (sg_hbm, sg_ref), (long_hbm, long_ref),
            (x_hbm, x_ref), (band_hbm, band_ref), (win_hbm, win_ref), (wout_hbm, wout_ref),
        ))
    ]
    for copy in operands:
        copy.start()

    def row_at(by):
        return lax.rem(me + (by + rows_n), rows_n)

    def col_at(by):
        return lax.rem(mc + by, cols_n)

    barrier = pltpu.get_barrier_semaphore()
    if reduce_here:
        def greet(k, carry):
            pl.semaphore_signal(barrier, inc=1, device_id={"row": row_at(k)}, device_id_type=MESH)
            return carry
        lax.fori_loop(1, rows_n, greet, 0)
        expected = rows_n - 1
    else:
        for d in DISTANCES:
            pl.semaphore_signal(barrier, inc=1, device_id={"row": row_at(d)}, device_id_type=MESH)
        expected = len(DISTANCES)
    for k in range(1, cols_n):
        pl.semaphore_signal(barrier, inc=1, device_id={"col": col_at(k)}, device_id_type=MESH)
    expected += cols_n - 1

    def slots_of(reader, owner):
        low, high = jnp.int32(0), jnp.int32(0)
        for s in range(SLOTS):
            match = (lax.div(src_ref[reader, s], nb) == owner).astype(jnp.int32)
            high = jnp.maximum(high, match * s)
            low = jnp.maximum(low, match * (SLOTS - 1 - s))
        low = SLOTS - 1 - low
        return low, high

    for copy in operands[:3]:
        copy.wait()
    served, read = [], []
    for d in DISTANCES:
        reader = row_at(-d)
        served.append([
            jnp.clip(src_ref[reader, s] - me * nb, 0, nb - 1) for s in slots_of(reader, me)
        ])
        read.append([
            (s, jnp.clip(rows_ref[0, s], 0, nb - 1), (s < count_ref[me]).astype(F32))
            for s in slots_of(me, row_at(d))
        ])

    for copy in operands[3:5]:
        copy.wait()
    for r in range(nb):
        sb[r] = sg_ref[:, lanes(r)].astype(wire)
    for pos in range(6):
        for rank in range(2):
            s, row, live = read[pos][rank]
            gs[pos, rank] = (live * nn(sb[row].astype(BF16), long_ref[s])).astype(wire)
    for copy in operands[5:7]:
        copy.wait()
    gs[BEFORE, 2] = nn(sg_ref[:, lanes(0)], band_ref[0, 0]).astype(wire)
    gs[BEYOND, 2] = nn(sg_ref[:, lanes(nb - 1)], band_ref[nb - 1, 2]).astype(wire)
    for r in range(nb):
        xb[r] = x_ref[:, lanes(r)]
    for pos in range(6):
        for rank in range(2):
            xs[pos, rank] = xb[served[pos][rank]]
    xs[BEFORE, 2] = xb[nb - 1]
    xs[BEYOND, 2] = xb[0]

    pl.semaphore_wait(barrier, expected)

    def swap(src, dst, ss, rs, pos, to):
        span = pl.ds(0, blocks_sent(pos))
        return pltpu.make_async_remote_copy(
            src_ref=src.at[pos, span], dst_ref=dst.at[pos, span],
            send_sem=ss.at[pos], recv_sem=rs.at[pos],
            device_id={"row": to}, device_id_type=MESH,
        )

    g_copies = [swap(gs, gr, g_ss, g_rs, pos, row_at(d)) for pos, d in enumerate(DISTANCES)]
    x_copies = [swap(xs, xr, x_ss, x_rs, pos, row_at(-d)) for pos, d in enumerate(DISTANCES)]
    for copy in g_copies + x_copies:
        copy.start()

    def three(r):
        start = (r - 1) * BLK
        return pl.ds(start if isinstance(r, int) else pl.multiple_of(start, BLK), 3 * BLK)

    def inner(body):
        lax.fori_loop(1, nb - 1, lambda r, c: (body(r), c)[1], 0, unroll=7)

    def g_band(r):
        blocks = jnp.concatenate([band_ref[r - 1, 2], band_ref[r, 1], band_ref[r + 1, 0]], 0)
        gacc[r] = nn(sg_ref[:, three(r)], blocks)

    def z_band(r):
        blocks = jnp.concatenate([band_ref[r, 0], band_ref[r, 1], band_ref[r, 2]], 1)
        zacc[r] = nt(x_ref[:, three(r)], blocks)

    last = nb - 1
    inner(g_band)
    gacc[0] = nn(sg_ref[:, lanes(0)], band_ref[0, 1]) + nn(sg_ref[:, lanes(1)], band_ref[1, 0])
    gacc[last] = nn(sg_ref[:, lanes(last)], band_ref[last, 1]) + nn(sg_ref[:, lanes(last - 1)], band_ref[last - 1, 2])

    for copy in g_copies:
        copy.wait_recv()
    gacc[0] += gr[BEYOND, 2].astype(F32)
    gacc[nb - 1] += gr[BEFORE, 2].astype(F32)

    def g_long(r, carry):
        total = gacc[r]
        for pos in range(6):
            for rank in range(2):
                total += (served[pos][rank] == r).astype(F32) * gr[pos, rank].astype(F32)
        g2[mc, :, lanes(r)] = total.astype(BF16).astype(wire)
        return carry

    lax.fori_loop(0, nb, g_long, 0, unroll=4)

    def g_share(k):
        return pltpu.make_async_remote_copy(
            src_ref=g2.at[mc], dst_ref=g2.at[mc],
            send_sem=gc_ss.at[k - 1], recv_sem=gc_rs.at[k - 1],
            device_id={"col": col_at(k)}, device_id_type=MESH,
        )

    def g_arrives(k):
        return pltpu.make_async_remote_copy(
            src_ref=g2.at[mc], dst_ref=g2.at[col_at(cols_n - k)],
            send_sem=gc_ss.at[k - 1], recv_sem=gc_rs.at[k - 1],
            device_id={"col": col_at(k)}, device_id_type=MESH,
        )

    g_shares = [g_share(k) for k in range(1, cols_n)]
    for copy in g_shares:
        copy.start()

    inner(z_band)
    zacc[0] = nt(xb[0], band_ref[0, 1]) + nt(xb[1], band_ref[0, 2])
    zacc[last] = nt(xb[last - 1], band_ref[last, 0]) + nt(xb[last], band_ref[last, 1])

    for copy in operands[7:]:
        copy.wait()
    win_t = win_ref[...].astype(F32).T.astype(BF16)
    out_f = jnp.zeros((wout_ref.shape[0], hidden), F32)
    for c in range(cols_n):
        out_f += (mc == c).astype(F32) * wout_ref[:, c * hidden:(c + 1) * hidden].astype(F32)
    out_t = out_f.astype(BF16)
    my_out = out_f.T.astype(BF16)
    first_ref[...] = jnp.zeros_like(first_ref)
    second_ref[...] = jnp.zeros_like(second_ref)

    for copy in x_copies:
        copy.wait_recv()
    for pos in range(6):
        for rank in range(2):
            s, row, live = read[pos][rank]
            contrib[2 * pos + rank] = nt(xr[pos, rank], long_ref[s])
    zacc[0] += nt(xr[BEFORE, 2], band_ref[0, 0])
    zacc[nb - 1] += nt(xr[BEYOND, 2], band_ref[nb - 1, 2])

    def z_long(r, carry):
        total = zacc[r]
        for pos in range(6):
            for rank in range(2):
                s, row, live = read[pos][rank]
                total += (live * (row == r).astype(F32)) * contrib[2 * pos + rank]
        z[:, lanes(r)] = total.astype(BF16)
        return carry

    lax.fori_loop(0, nb, z_long, 0, unroll=2)

    tile = 4 * BLK
    tiles = nodes // tile

    def tile_at(t):
        return pl.ds(t * tile, tile)

    def p_share(k, t):
        return pltpu.make_async_remote_copy(
            src_ref=part_out.at[col_at(k), :, tile_at(t)], dst_ref=part_in.at[k - 1, :, tile_at(t)],
            send_sem=p_ss.at[k - 1, t], recv_sem=p_rs.at[k - 1, t],
            device_id={"col": col_at(k)}, device_id_type=MESH,
        )

    for k in range(1, cols_n):
        g_arrives(k).wait_recv()
    p_shares = []
    for t in range(tiles):
        v = nn(win_t, z[:, tile_at(t)])
        sig = 0.5 * jnp.tanh(0.5 * v) + 0.5
        h = (v * sig).astype(BF16)
        p = nn(out_t, h)
        for c in range(cols_n):
            part[c, :, tile_at(t)] = p[c * cc:(c + 1) * cc]
            part_out[c, :, tile_at(t)] = p[c * cc:(c + 1) * cc].astype(wire)
        for k in range(1, cols_n):
            p_shares.append(p_share(k, t))
            p_shares[-1].start()
        g = g2[:, :, tile_at(t)].reshape(cols_n * cc, tile).astype(BF16)
        second_ref[...] += nt(g, h)
        ds = (nn(my_out, g) * (sig * (1.0 + v * (1.0 - sig)))).astype(BF16)
        first_ref[...] += nt(z[:, tile_at(t)], ds)

    if reduce_here:
        fr = first_ref.shape[0] // rows_n
        sr = second_ref.shape[0] // rows_n
        for j in range(rows_n):
            mine = [first_ref[j * fr:(j + 1) * fr], second_ref[j * sr:(j + 1) * sr]]
            if red.shape[1] > fr + sr:
                mine.append(jnp.zeros((red.shape[1] - fr - sr, hidden), F32))
            red[j] = jnp.concatenate(mine, 0).astype(red.dtype)

        def red_copy(k):
            return pltpu.make_async_remote_copy(
                src_ref=red.at[row_at(k)], dst_ref=red_in.at[k - 1],
                send_sem=red_ss.at[k - 1], recv_sem=red_rs.at[k - 1],
                device_id={"row": row_at(k)}, device_id_type=MESH,
            )

        def all_copy(k, slot):
            return pltpu.make_async_remote_copy(
                src_ref=summed.at[me], dst_ref=summed.at[slot],
                send_sem=all_ss.at[k - 1], recv_sem=all_rs.at[k - 1],
                device_id={"row": row_at(k)}, device_id_type=MESH,
            )

        def over_peers(body):
            lax.fori_loop(1, rows_n, lambda k, c: (body(k), c)[1], 0)

        over_peers(lambda k: red_copy(k).start())

    for copy in p_shares:
        copy.wait_recv()

    def class_block(r, carry):
        total = part[mc, :, lanes(r)]
        for k in range(cols_n - 1):
            total += part_in[k, :, lanes(r)].astype(F32)
        cls[r] = total.astype(BF16).astype(wire)
        return carry

    lax.fori_loop(0, nb, class_block, 0, unroll=4)

    for pos in range(6):
        for rank in range(2):
            cs[pos, rank] = cls[served[pos][rank]]
    cs[BEFORE, 2] = cls[nb - 1]
    cs[BEYOND, 2] = cls[0]
    c_copies = [swap(cs, cr, c_ss, c_rs, pos, row_at(-d)) for pos, d in enumerate(DISTANCES)]
    for copy in c_copies:
        copy.start()

    def s_band(r):
        values = jnp.concatenate([cls[r - 1], cls[r], cls[r + 1]], 1).astype(BF16)
        blocks = jnp.concatenate([band_ref[r, 0], band_ref[r, 1], band_ref[r, 2]], 1)
        gacc[r] = nt(values, blocks)

    inner(s_band)
    gacc[0] = nt(cls[0].astype(BF16), band_ref[0, 1]) + nt(cls[1].astype(BF16), band_ref[0, 2])
    gacc[last] = nt(cls[last - 1].astype(BF16), band_ref[last, 0]) + nt(cls[last].astype(BF16), band_ref[last, 1])

    if reduce_here:
        over_peers(lambda k: red_copy(k).wait_recv())
        total = red[me].astype(F32)
        for k in range(rows_n - 1):
            total += red_in[k].astype(F32)
        summed[me] = total.astype(summed.dtype)
        over_peers(lambda k: all_copy(k, me).start())

    for copy in c_copies:
        copy.wait_recv()
    for pos in range(6):
        for rank in range(2):
            s, row, live = read[pos][rank]
            contrib[2 * pos + rank, 0:cc] = nt(cr[pos, rank].astype(BF16), long_ref[s])
    gacc[0] += nt(cr[BEFORE, 2].astype(BF16), band_ref[0, 0])
    gacc[nb - 1] += nt(cr[BEYOND, 2].astype(BF16), band_ref[nb - 1, 2])

    def s_long(r, carry):
        total = gacc[r]
        for pos in range(6):
            for rank in range(2):
                s, row, live = read[pos][rank]
                total += (live * (row == r).astype(F32)) * contrib[2 * pos + rank, 0:cc]
        scores_ref[:, lanes(r)] = total.astype(BF16)
        return carry

    lax.fori_loop(0, nb, s_long, 0, unroll=4)

    if reduce_here:
        over_peers(lambda k: all_copy(k, row_at(-k)).wait_recv())
        for j in range(rows_n):
            final = summed[j].astype(F32)
            first_ref[j * fr:(j + 1) * fr] = final[0:fr]
            second_ref[j * sr:(j + 1) * sr] = final[fr:fr + sr]
        over_peers(lambda k: red_copy(k).wait_send())
        over_peers(lambda k: all_copy(k, me).wait_send())

    for copy in x_copies + g_copies + c_copies + g_shares + p_shares:
        copy.wait_send()


def local(
    features, weight_in, weight_out, score_grad, band_blocks, long_blocks, long_rows, long_sources, long_counts,
):
    rows_n = lax.axis_size("row")
    cols_n = lax.axis_size("col")
    feats, nodes = features.shape
    nb = nodes // BLK
    hidden = weight_in.shape[1]
    cc = score_grad.shape[0]
    classes = weight_out.shape[1]
    wire = BF16 if cc % 16 == 0 else F32
    reduce_here = feats % (8 * rows_n) == 0 and classes % rows_n == 0 and hidden % BLK == 0
    chunk = -(-((feats + classes) // rows_n) // 16) * 16 if reduce_here else 16
    slices = rows_n if reduce_here else 1
    peers = max(slices - 1, 1)
    dma = pltpu.SemaphoreType.DMA
    vmem = pl.BlockSpec(memory_space=pltpu.VMEM)
    scores, first, second = pl.pallas_call(
        functools.partial(kernel, rows_n, cols_n, reduce_here),
        out_shape=(
            jax.ShapeDtypeStruct((cc, nodes), BF16),
            jax.ShapeDtypeStruct((feats, hidden), F32),
            jax.ShapeDtypeStruct((classes, hidden), F32),
        ),
        in_specs=[pl.BlockSpec(memory_space=pl.ANY)] * 9,
        out_specs=(vmem, vmem, vmem),
        scratch_shapes=[
            pltpu.VMEM(features.shape, BF16),
            pltpu.VMEM(weight_in.shape, BF16),
            pltpu.VMEM(weight_out.shape[::-1], BF16),
            pltpu.VMEM(score_grad.shape, BF16),
            pltpu.VMEM(band_blocks.shape, BF16),
            pltpu.VMEM(long_blocks.shape, BF16),
            pltpu.SMEM(long_rows.shape, jnp.int32),
            pltpu.SMEM(long_sources.shape, jnp.int32),
            pltpu.SMEM(long_counts.shape, jnp.int32),
            dma((9,)),
            pltpu.VMEM((nb, feats, BLK), BF16),
            pltpu.VMEM((nb, cc, BLK), wire),
            pltpu.VMEM((6, 3, feats, BLK), BF16),
            pltpu.VMEM((6, 3, feats, BLK), BF16),
            pltpu.VMEM((6, 3, cc, BLK), wire),
            pltpu.VMEM((6, 3, cc, BLK), wire),
            pltpu.VMEM((6, 3, cc, BLK), wire),
            pltpu.VMEM((6, 3, cc, BLK), wire),
            pltpu.VMEM((nb, feats, BLK), F32),
            pltpu.VMEM((SLOTS, feats, BLK), F32),
            pltpu.VMEM((feats, nodes), BF16),
            pltpu.VMEM((nb, cc, BLK), F32),
            pltpu.VMEM((cols_n, cc, nodes), wire),
            pltpu.VMEM((cols_n, cc, nodes), F32),
            pltpu.VMEM((cols_n, cc, nodes), wire),
            pltpu.VMEM((cols_n - 1, cc, nodes), wire),
            pltpu.VMEM((nb, cc, BLK), wire),
            pltpu.VMEM((slices, chunk, hidden), BF16),
            pltpu.VMEM((peers, chunk, hidden), BF16),
            pltpu.VMEM((slices, chunk, hidden), BF16),
            dma((6,)), dma((6,)), dma((6,)), dma((6,)), dma((6,)), dma((6,)),
            dma((cols_n - 1,)), dma((cols_n - 1,)), dma((cols_n - 1, nodes // (4 * BLK))), dma((cols_n - 1, nodes // (4 * BLK))),
            dma((peers,)), dma((peers,)), dma((peers,)), dma((peers,)),
        ],
        compiler_params=pltpu.CompilerParams(
            collective_id=0, has_side_effects=True, vmem_limit_bytes=40 * 1024 * 1024
        ),
    )(features, weight_in, weight_out.T, score_grad, band_blocks, long_blocks, long_rows, long_sources, long_counts)
    second = second.T
    if not reduce_here:
        first, second = lax.psum((first, second), "row")
    return scores, first, second


def solution(mesh):
    return jax.shard_map(
        local,
        mesh=mesh,
        in_specs=(
            P(None, "row"),
            P(None, "col"),
            P(),
            P("col", "row"),
            P("row", None, None, None),
            P("row", None, None),
            P("row", None),
            P(),
            P(),
        ),
        out_specs=(P("col", "row"), P(None, "col"), P("col", None)),
        check_vma=False,
    )
```

```python
import functools

import jax
import jax.numpy as jnp
from jax import lax
from jax.experimental import pallas as pl
from jax.experimental.pallas import tpu as pltpu
from jax.sharding import PartitionSpec as P

BLK = 128
SLOTS = 12
DISTANCES = (-3, -2, -1, 1, 2, 3)
BEFORE = DISTANCES.index(-1)
BEYOND = DISTANCES.index(1)
NEAR_FIRST = sorted(range(6), key=lambda pos: abs(DISTANCES[pos]))
MESH = pl.DeviceIdType.MESH
F32 = jnp.float32
BF16 = jnp.bfloat16


def nn(a, b):
    return lax.dot_general(a, b, (((1,), (0,)), ((), ())), preferred_element_type=F32)


def nt(a, b):
    return lax.dot_general(a, b, (((1,), (1,)), ((), ())), preferred_element_type=F32)


def lanes(block):
    if isinstance(block, int):
        return pl.ds(block * BLK, BLK)
    return pl.ds(pl.multiple_of(block * BLK, BLK), BLK)


def blocks_sent(pos):
    return 3 if pos in (BEFORE, BEYOND) else 2


def kernel(
    rows_n, cols_n, reduce_here,
    x_hbm, win_hbm, wout_hbm, sg_hbm, band_hbm, long_hbm, rows_hbm, src_hbm, count_hbm,
    scores_ref, first_ref, second_ref,
    x_ref, win_ref, wout_ref, sg_ref, band_ref, long_ref, rows_ref, src_ref, count_ref, in_sem,
    xb, sb, xs, xr, gs, gr, cs, cr, zacc, contrib, z, gacc, g2, part, part_out, part_in, cls, red, red_in, summed,
    x_ss, x_rs, g_ss, g_rs, c_ss, c_rs, gc_ss, gc_rs, p_ss, p_rs, red_ss, red_rs, all_ss, all_rs,
):
    me = lax.axis_index("row")
    mc = lax.axis_index("col")
    nodes = x_ref.shape[1]
    nb = nodes // BLK
    hidden = win_ref.shape[1]
    cc = sg_ref.shape[0]
    wire = gs.dtype

    operands = [
        pltpu.make_async_copy(src, dst, in_sem.at[i])
        for i, (src, dst) in enumerate((
            (rows_hbm, rows_ref), (src_hbm, src_ref), (count_hbm, count_ref), (sg_hbm, sg_ref), (long_hbm, long_ref),
            (x_hbm, x_ref), (band_hbm, band_ref), (win_hbm, win_ref), (wout_hbm, wout_ref),
        ))
    ]
    for copy in operands:
        copy.start()

    def row_at(by):
        return lax.rem(me + (by + rows_n), rows_n)

    def col_at(by):
        return lax.rem(mc + by, cols_n)

    barrier = pltpu.get_barrier_semaphore()
    if reduce_here:
        def greet(k, carry):
            pl.semaphore_signal(barrier, inc=1, device_id={"row": row_at(k)}, device_id_type=MESH)
            return carry
        lax.fori_loop(1, rows_n, greet, 0)
        expected = rows_n - 1
    else:
        for d in DISTANCES:
            pl.semaphore_signal(barrier, inc=1, device_id={"row": row_at(d)}, device_id_type=MESH)
        expected = len(DISTANCES)
    for k in range(1, cols_n):
        pl.semaphore_signal(barrier, inc=1, device_id={"col": col_at(k)}, device_id_type=MESH)
    expected += cols_n - 1

    def slots_of(reader, owner):
        low, high = jnp.int32(0), jnp.int32(0)
        for s in range(SLOTS):
            match = (lax.div(src_ref[reader, s], nb) == owner).astype(jnp.int32)
            high = jnp.maximum(high, match * s)
            low = jnp.maximum(low, match * (SLOTS - 1 - s))
        low = SLOTS - 1 - low
        return low, high

    for copy in operands[:3]:
        copy.wait()
    served, read = [], []
    for d in DISTANCES:
        reader = row_at(-d)
        served.append([
            jnp.clip(src_ref[reader, s] - me * nb, 0, nb - 1) for s in slots_of(reader, me)
        ])
        read.append([
            (s, jnp.clip(rows_ref[0, s], 0, nb - 1), (s < count_ref[me]).astype(F32))
            for s in slots_of(me, row_at(d))
        ])

    for copy in operands[3:5]:
        copy.wait()
    for r in range(nb):
        sb[r] = sg_ref[:, lanes(r)].astype(wire)
    for pos in range(6):
        for rank in range(2):
            s, row, live = read[pos][rank]
            gs[pos, rank] = (live * nn(sb[row].astype(BF16), long_ref[s])).astype(wire)
    for copy in operands[5:7]:
        copy.wait()
    gs[BEFORE, 2] = nn(sg_ref[:, lanes(0)], band_ref[0, 0]).astype(wire)
    gs[BEYOND, 2] = nn(sg_ref[:, lanes(nb - 1)], band_ref[nb - 1, 2]).astype(wire)
    for r in range(nb):
        xb[r] = x_ref[:, lanes(r)]
    for pos in range(6):
        for rank in range(2):
            xs[pos, rank] = xb[served[pos][rank]]
    xs[BEFORE, 2] = xb[nb - 1]
    xs[BEYOND, 2] = xb[0]

    pl.semaphore_wait(barrier, expected)

    def swap(src, dst, ss, rs, pos, to):
        span = pl.ds(0, blocks_sent(pos))
        return pltpu.make_async_remote_copy(
            src_ref=src.at[pos, span], dst_ref=dst.at[pos, span],
            send_sem=ss.at[pos], recv_sem=rs.at[pos],
            device_id={"row": to}, device_id_type=MESH,
        )

    g_copies = [swap(gs, gr, g_ss, g_rs, pos, row_at(d)) for pos, d in enumerate(DISTANCES)]
    x_copies = [swap(xs, xr, x_ss, x_rs, pos, row_at(-d)) for pos, d in enumerate(DISTANCES)]
    for copies in (g_copies, x_copies):
        for pos in reversed(NEAR_FIRST):
            copies[pos].start()

    def three(r):
        start = (r - 1) * BLK
        return pl.ds(start if isinstance(r, int) else pl.multiple_of(start, BLK), 3 * BLK)

    def inner(body):
        lax.fori_loop(1, nb - 1, lambda r, c: (body(r), c)[1], 0, unroll=7)

    def g_band(r):
        blocks = jnp.concatenate([band_ref[r - 1, 2], band_ref[r, 1], band_ref[r + 1, 0]], 0)
        gacc[r] = nn(sg_ref[:, three(r)], blocks)

    def z_band(r):
        blocks = jnp.concatenate([band_ref[r, 0], band_ref[r, 1], band_ref[r, 2]], 1)
        zacc[r] = nt(x_ref[:, three(r)], blocks)

    last = nb - 1
    inner(g_band)
    gacc[0] = nn(sg_ref[:, lanes(0)], band_ref[0, 1]) + nn(sg_ref[:, lanes(1)], band_ref[1, 0])
    gacc[last] = nn(sg_ref[:, lanes(last)], band_ref[last, 1]) + nn(sg_ref[:, lanes(last - 1)], band_ref[last - 1, 2])

    for copy in g_copies:
        copy.wait_recv()
    gacc[0] += gr[BEYOND, 2].astype(F32)
    gacc[nb - 1] += gr[BEFORE, 2].astype(F32)

    def g_long(r, carry):
        total = gacc[r]
        for pos in range(6):
            for rank in range(2):
                total += (served[pos][rank] == r).astype(F32) * gr[pos, rank].astype(F32)
        g2[mc, :, lanes(r)] = total.astype(BF16).astype(wire)
        return carry

    lax.fori_loop(0, nb, g_long, 0, unroll=4)

    def g_share(k):
        return pltpu.make_async_remote_copy(
            src_ref=g2.at[mc], dst_ref=g2.at[mc],
            send_sem=gc_ss.at[k - 1], recv_sem=gc_rs.at[k - 1],
            device_id={"col": col_at(k)}, device_id_type=MESH,
        )

    def g_arrives(k):
        return pltpu.make_async_remote_copy(
            src_ref=g2.at[mc], dst_ref=g2.at[col_at(cols_n - k)],
            send_sem=gc_ss.at[k - 1], recv_sem=gc_rs.at[k - 1],
            device_id={"col": col_at(k)}, device_id_type=MESH,
        )

    g_shares = [g_share(k) for k in range(1, cols_n)]
    for copy in g_shares:
        copy.start()

    inner(z_band)
    zacc[0] = nt(xb[0], band_ref[0, 1]) + nt(xb[1], band_ref[0, 2])
    zacc[last] = nt(xb[last - 1], band_ref[last, 0]) + nt(xb[last], band_ref[last, 1])

    for copy in operands[7:]:
        copy.wait()
    win_t = win_ref[...].astype(F32).T.astype(BF16)
    out_f = jnp.zeros((wout_ref.shape[0], hidden), F32)
    for c in range(cols_n):
        out_f += (mc == c).astype(F32) * wout_ref[:, c * hidden:(c + 1) * hidden].astype(F32)
    out_t = out_f.astype(BF16)
    my_out = out_f.T.astype(BF16)
    first_ref[...] = jnp.zeros_like(first_ref)
    second_ref[...] = jnp.zeros_like(second_ref)

    for pos in NEAR_FIRST:
        x_copies[pos].wait_recv()
        for rank in range(2):
            contrib[rank] = nt(xr[pos, rank], long_ref[read[pos][rank][0]])
        if pos == BEFORE:
            zacc[0] += nt(xr[pos, 2], band_ref[0, 0])
        if pos == BEYOND:
            zacc[last] += nt(xr[pos, 2], band_ref[last, 2])

        def z_long(r, carry, pos=pos):
            total = zacc[r]
            for rank in range(2):
                s, row, live = read[pos][rank]
                total += (live * (row == r).astype(F32)) * contrib[rank]
            if pos == NEAR_FIRST[-1]:
                z[:, lanes(r)] = total.astype(BF16)
            else:
                zacc[r] = total
            return carry

        lax.fori_loop(0, nb, z_long, 0, unroll=4)

    tile = 4 * BLK
    tiles = nodes // tile

    def tile_at(t):
        return pl.ds(t * tile, tile)

    def p_share(k, t):
        return pltpu.make_async_remote_copy(
            src_ref=part_out.at[col_at(k), :, tile_at(t)], dst_ref=part_in.at[k - 1, :, tile_at(t)],
            send_sem=p_ss.at[k - 1, t], recv_sem=p_rs.at[k - 1, t],
            device_id={"col": col_at(k)}, device_id_type=MESH,
        )

    for k in range(1, cols_n):
        g_arrives(k).wait_recv()
    p_shares = []
    for t in range(tiles):
        v = nn(win_t, z[:, tile_at(t)])
        sig = 0.5 * jnp.tanh(0.5 * v) + 0.5
        h = (v * sig).astype(BF16)
        p = nn(out_t, h)
        for c in range(cols_n):
            part[c, :, tile_at(t)] = p[c * cc:(c + 1) * cc]
            part_out[c, :, tile_at(t)] = p[c * cc:(c + 1) * cc].astype(wire)
        for k in range(1, cols_n):
            p_shares.append(p_share(k, t))
            p_shares[-1].start()
        g = g2[:, :, tile_at(t)].reshape(cols_n * cc, tile).astype(BF16)
        second_ref[...] += nt(g, h)
        ds = (nn(my_out, g) * (sig * (1.0 + v * (1.0 - sig)))).astype(BF16)
        first_ref[...] += nt(z[:, tile_at(t)], ds)

    if reduce_here:
        fr = first_ref.shape[0] // rows_n
        sr = second_ref.shape[0] // rows_n
        for j in range(rows_n):
            mine = [first_ref[j * fr:(j + 1) * fr], second_ref[j * sr:(j + 1) * sr]]
            if red.shape[1] > fr + sr:
                mine.append(jnp.zeros((red.shape[1] - fr - sr, hidden), F32))
            red[j] = jnp.concatenate(mine, 0).astype(red.dtype)

        def red_copy(k):
            return pltpu.make_async_remote_copy(
                src_ref=red.at[row_at(k)], dst_ref=red_in.at[k - 1],
                send_sem=red_ss.at[k - 1], recv_sem=red_rs.at[k - 1],
                device_id={"row": row_at(k)}, device_id_type=MESH,
            )

        def all_copy(k, slot):
            return pltpu.make_async_remote_copy(
                src_ref=summed.at[me], dst_ref=summed.at[slot],
                send_sem=all_ss.at[k - 1], recv_sem=all_rs.at[k - 1],
                device_id={"row": row_at(k)}, device_id_type=MESH,
            )

        def over_peers(body):
            lax.fori_loop(1, rows_n, lambda k, c: (body(k), c)[1], 0)

        over_peers(lambda k: red_copy(k).start())

    for copy in p_shares:
        copy.wait_recv()

    def class_block(r, carry):
        total = part[mc, :, lanes(r)]
        for k in range(cols_n - 1):
            total += part_in[k, :, lanes(r)].astype(F32)
        cls[r] = total.astype(BF16).astype(wire)
        return carry

    lax.fori_loop(0, nb, class_block, 0, unroll=4)

    for pos in range(6):
        for rank in range(2):
            cs[pos, rank] = cls[served[pos][rank]]
    cs[BEFORE, 2] = cls[nb - 1]
    cs[BEYOND, 2] = cls[0]
    c_copies = [swap(cs, cr, c_ss, c_rs, pos, row_at(-d)) for pos, d in enumerate(DISTANCES)]
    for copy in c_copies:
        copy.start()

    def s_band(r):
        values = jnp.concatenate([cls[r - 1], cls[r], cls[r + 1]], 1).astype(BF16)
        blocks = jnp.concatenate([band_ref[r, 0], band_ref[r, 1], band_ref[r, 2]], 1)
        gacc[r] = nt(values, blocks)

    inner(s_band)
    gacc[0] = nt(cls[0].astype(BF16), band_ref[0, 1]) + nt(cls[1].astype(BF16), band_ref[0, 2])
    gacc[last] = nt(cls[last - 1].astype(BF16), band_ref[last, 0]) + nt(cls[last].astype(BF16), band_ref[last, 1])

    if reduce_here:
        over_peers(lambda k: red_copy(k).wait_recv())
        total = red[me].astype(F32)
        for k in range(rows_n - 1):
            total += red_in[k].astype(F32)
        summed[me] = total.astype(summed.dtype)
        over_peers(lambda k: all_copy(k, me).start())

    for copy in c_copies:
        copy.wait_recv()
    for pos in range(6):
        for rank in range(2):
            s, row, live = read[pos][rank]
            contrib[2 * pos + rank, 0:cc] = nt(cr[pos, rank].astype(BF16), long_ref[s])
    gacc[0] += nt(cr[BEFORE, 2].astype(BF16), band_ref[0, 0])
    gacc[nb - 1] += nt(cr[BEYOND, 2].astype(BF16), band_ref[nb - 1, 2])

    def s_long(r, carry):
        total = gacc[r]
        for pos in range(6):
            for rank in range(2):
                s, row, live = read[pos][rank]
                total += (live * (row == r).astype(F32)) * contrib[2 * pos + rank, 0:cc]
        scores_ref[:, lanes(r)] = total.astype(BF16)
        return carry

    lax.fori_loop(0, nb, s_long, 0, unroll=4)

    if reduce_here:
        over_peers(lambda k: all_copy(k, row_at(-k)).wait_recv())
        for j in range(rows_n):
            final = summed[j].astype(F32)
            first_ref[j * fr:(j + 1) * fr] = final[0:fr]
            second_ref[j * sr:(j + 1) * sr] = final[fr:fr + sr]
        over_peers(lambda k: red_copy(k).wait_send())
        over_peers(lambda k: all_copy(k, me).wait_send())

    for copy in x_copies + g_copies + c_copies + g_shares + p_shares:
        copy.wait_send()


def local(
    features, weight_in, weight_out, score_grad, band_blocks, long_blocks, long_rows, long_sources, long_counts,
):
    rows_n = lax.axis_size("row")
    cols_n = lax.axis_size("col")
    feats, nodes = features.shape
    nb = nodes // BLK
    hidden = weight_in.shape[1]
    cc = score_grad.shape[0]
    classes = weight_out.shape[1]
    wire = BF16 if cc % 16 == 0 else F32
    reduce_here = feats % (8 * rows_n) == 0 and classes % rows_n == 0 and hidden % BLK == 0
    chunk = -(-((feats + classes) // rows_n) // 16) * 16 if reduce_here else 16
    slices = rows_n if reduce_here else 1
    peers = max(slices - 1, 1)
    dma = pltpu.SemaphoreType.DMA
    vmem = pl.BlockSpec(memory_space=pltpu.VMEM)
    scores, first, second = pl.pallas_call(
        functools.partial(kernel, rows_n, cols_n, reduce_here),
        out_shape=(
            jax.ShapeDtypeStruct((cc, nodes), BF16),
            jax.ShapeDtypeStruct((feats, hidden), F32),
            jax.ShapeDtypeStruct((classes, hidden), F32),
        ),
        in_specs=[pl.BlockSpec(memory_space=pltpu.HBM)] * 9,
        out_specs=(vmem, vmem, vmem),
        scratch_shapes=[
            pltpu.VMEM(features.shape, BF16),
            pltpu.VMEM(weight_in.shape, BF16),
            pltpu.VMEM(weight_out.shape[::-1], BF16),
            pltpu.VMEM(score_grad.shape, BF16),
            pltpu.VMEM(band_blocks.shape, BF16),
            pltpu.VMEM(long_blocks.shape, BF16),
            pltpu.SMEM(long_rows.shape, jnp.int32),
            pltpu.SMEM(long_sources.shape, jnp.int32),
            pltpu.SMEM(long_counts.shape, jnp.int32),
            dma((9,)),
            pltpu.VMEM((nb, feats, BLK), BF16),
            pltpu.VMEM((nb, cc, BLK), wire),
            pltpu.VMEM((6, 3, feats, BLK), BF16),
            pltpu.VMEM((6, 3, feats, BLK), BF16),
            pltpu.VMEM((6, 3, cc, BLK), wire),
            pltpu.VMEM((6, 3, cc, BLK), wire),
            pltpu.VMEM((6, 3, cc, BLK), wire),
            pltpu.VMEM((6, 3, cc, BLK), wire),
            pltpu.VMEM((nb, feats, BLK), F32),
            pltpu.VMEM((SLOTS, feats, BLK), F32),
            pltpu.VMEM((feats, nodes), BF16),
            pltpu.VMEM((nb, cc, BLK), F32),
            pltpu.VMEM((cols_n, cc, nodes), wire),
            pltpu.VMEM((cols_n, cc, nodes), F32),
            pltpu.VMEM((cols_n, cc, nodes), wire),
            pltpu.VMEM((cols_n - 1, cc, nodes), wire),
            pltpu.VMEM((nb, cc, BLK), wire),
            pltpu.VMEM((slices, chunk, hidden), BF16),
            pltpu.VMEM((peers, chunk, hidden), BF16),
            pltpu.VMEM((slices, chunk, hidden), BF16),
            dma((6,)), dma((6,)), dma((6,)), dma((6,)), dma((6,)), dma((6,)),
            dma((cols_n - 1,)), dma((cols_n - 1,)), dma((cols_n - 1, nodes // (4 * BLK))), dma((cols_n - 1, nodes // (4 * BLK))),
            dma((peers,)), dma((peers,)), dma((peers,)), dma((peers,)),
        ],
        compiler_params=pltpu.CompilerParams(
            collective_id=0, has_side_effects=True, vmem_limit_bytes=60 * 1024 * 1024
        ),
    )(features, weight_in, weight_out.T, score_grad, band_blocks, long_blocks, long_rows, long_sources, long_counts)
    second = second.T
    if not reduce_here:
        first, second = lax.psum((first, second), "row")
    return scores, first, second


def solution(mesh):
    return jax.shard_map(
        local,
        mesh=mesh,
        in_specs=(
            P(None, "row"),
            P(None, "col"),
            P(),
            P("col", "row"),
            P("row", None, None, None),
            P("row", None, None),
            P("row", None),
            P(),
            P(),
        ),
        out_specs=(P("col", "row"), P(None, "col"), P("col", None)),
        check_vma=False,
    )
```

```python
import functools

import jax
import jax.numpy as jnp
from jax import lax
from jax.experimental import pallas as pl
from jax.experimental.pallas import tpu as pltpu
from jax.sharding import PartitionSpec as P

BLK = 128
SLOTS = 12
DISTANCES = (-3, -2, -1, 1, 2, 3)
BEFORE = DISTANCES.index(-1)
BEYOND = DISTANCES.index(1)
NEAR_FIRST = sorted(range(6), key=lambda pos: abs(DISTANCES[pos]))
MESH = pl.DeviceIdType.MESH
F32 = jnp.float32
BF16 = jnp.bfloat16


def nn(a, b):
    return lax.dot_general(a, b, (((1,), (0,)), ((), ())), preferred_element_type=F32)


def nt(a, b):
    return lax.dot_general(a, b, (((1,), (1,)), ((), ())), preferred_element_type=F32)


def lanes(block):
    if isinstance(block, int):
        return pl.ds(block * BLK, BLK)
    return pl.ds(pl.multiple_of(block * BLK, BLK), BLK)


def blocks_sent(pos):
    return 3 if pos in (BEFORE, BEYOND) else 2


def kernel(
    rows_n, cols_n, reduce_here,
    x_hbm, win_hbm, wout_hbm, sg_hbm, band_hbm, long_hbm, rows_hbm, src_hbm, count_hbm,
    scores_ref, first_ref, second_ref,
    x_ref, win_ref, wout_ref, sg_ref, band_ref, long_ref, rows_ref, src_ref, count_ref, in_sem,
    xb, sb, xs, xr, gs, gr, cs, cr, zacc, contrib, z, gacc, g2, part, part_out, part_in, cls, red, pair_in, half, red_in, summed,
    x_ss, x_rs, g_ss, g_rs, c_ss, c_rs, gc_ss, gc_rs, p_ss, p_rs, red_ss, red_rs, all_ss, all_rs, pair_ss, pair_rs,
):
    me = lax.axis_index("row")
    mc = lax.axis_index("col")
    nodes = x_ref.shape[1]
    nb = nodes // BLK
    hidden = win_ref.shape[1]
    cc = sg_ref.shape[0]
    wire = gs.dtype

    operands = [
        pltpu.make_async_copy(src, dst, in_sem.at[i])
        for i, (src, dst) in enumerate((
            (rows_hbm, rows_ref), (src_hbm, src_ref), (count_hbm, count_ref), (sg_hbm, sg_ref), (long_hbm, long_ref),
            (x_hbm, x_ref), (band_hbm, band_ref), (win_hbm, win_ref), (wout_hbm, wout_ref),
        ))
    ]
    for copy in operands:
        copy.start()

    def row_at(by):
        return lax.rem(me + (by + rows_n), rows_n)

    def col_at(by):
        return lax.rem(mc + by, cols_n)

    barrier = pltpu.get_barrier_semaphore()
    greeted = {d % rows_n for d in DISTANCES}
    if reduce_here:
        greeted |= set(range(2, rows_n, 2))
    for k in sorted(greeted):
        pl.semaphore_signal(barrier, inc=1, device_id={"row": row_at(k)}, device_id_type=MESH)
    expected = len(greeted)
    for k in range(1, cols_n):
        pl.semaphore_signal(barrier, inc=1, device_id={"col": col_at(k)}, device_id_type=MESH)
    expected += cols_n - 1

    def slots_of(owners, owner):
        low, high = jnp.int32(0), jnp.int32(0)
        for s in range(SLOTS):
            high = jnp.where(owners[s] == owner, s, high)
            low = jnp.where(owners[SLOTS - 1 - s] == owner, SLOTS - 1 - s, low)
        return low, high

    def owners_of(reader):
        return [lax.div(src_ref[reader, s], nb) for s in range(SLOTS)]

    for copy in operands[:3]:
        copy.wait()
    my_owners = owners_of(me)
    served, read = [], []
    for d in DISTANCES:
        reader = row_at(-d)
        served.append([
            jnp.clip(src_ref[reader, s] - me * nb, 0, nb - 1) for s in slots_of(owners_of(reader), me)
        ])
        read.append([
            (s, jnp.clip(rows_ref[0, s], 0, nb - 1), (s < count_ref[me]).astype(F32))
            for s in slots_of(my_owners, row_at(d))
        ])

    for copy in operands[3:5]:
        copy.wait()
    for r in range(nb):
        sb[r] = sg_ref[:, lanes(r)].astype(wire)
    for pos in range(6):
        for rank in range(2):
            s, row, live = read[pos][rank]
            gs[pos, rank] = (live * nn(sb[row].astype(BF16), long_ref[s])).astype(wire)
    for copy in operands[5:7]:
        copy.wait()
    gs[BEFORE, 2] = nn(sg_ref[:, lanes(0)], band_ref[0, 0]).astype(wire)
    gs[BEYOND, 2] = nn(sg_ref[:, lanes(nb - 1)], band_ref[nb - 1, 2]).astype(wire)
    for r in range(nb):
        xb[r] = x_ref[:, lanes(r)]
    for pos in range(6):
        for rank in range(2):
            xs[pos, rank] = xb[served[pos][rank]]
    xs[BEFORE, 2] = xb[nb - 1]
    xs[BEYOND, 2] = xb[0]

    pl.semaphore_wait(barrier, expected)

    def swap(src, dst, ss, rs, pos, to):
        span = pl.ds(0, blocks_sent(pos))
        return pltpu.make_async_remote_copy(
            src_ref=src.at[pos, span], dst_ref=dst.at[pos, span],
            send_sem=ss.at[pos], recv_sem=rs.at[pos],
            device_id={"row": to}, device_id_type=MESH,
        )

    g_copies = [swap(gs, gr, g_ss, g_rs, pos, row_at(d)) for pos, d in enumerate(DISTANCES)]
    x_copies = [swap(xs, xr, x_ss, x_rs, pos, row_at(-d)) for pos, d in enumerate(DISTANCES)]
    for copies in (g_copies, x_copies):
        for pos in reversed(NEAR_FIRST):
            copies[pos].start()

    def three(r):
        start = (r - 1) * BLK
        return pl.ds(start if isinstance(r, int) else pl.multiple_of(start, BLK), 3 * BLK)

    def inner(body):
        lax.fori_loop(1, nb - 1, lambda r, c: (body(r), c)[1], 0, unroll=7)

    def g_band(r):
        blocks = jnp.concatenate([band_ref[r - 1, 2], band_ref[r, 1], band_ref[r + 1, 0]], 0)
        gacc[r] = nn(sg_ref[:, three(r)], blocks)

    def z_band(r):
        blocks = jnp.concatenate([band_ref[r, 0], band_ref[r, 1], band_ref[r, 2]], 1)
        zacc[r] = nt(x_ref[:, three(r)], blocks)

    last = nb - 1
    inner(g_band)
    gacc[0] = nn(sg_ref[:, lanes(0)], band_ref[0, 1]) + nn(sg_ref[:, lanes(1)], band_ref[1, 0])
    gacc[last] = nn(sg_ref[:, lanes(last)], band_ref[last, 1]) + nn(sg_ref[:, lanes(last - 1)], band_ref[last - 1, 2])

    for copy in g_copies:
        copy.wait_recv()
    gacc[0] += gr[BEYOND, 2].astype(F32)
    gacc[nb - 1] += gr[BEFORE, 2].astype(F32)

    def g_long(r, carry):
        total = gacc[r]
        for pos in range(6):
            for rank in range(2):
                total += (served[pos][rank] == r).astype(F32) * gr[pos, rank].astype(F32)
        g2[mc, :, lanes(r)] = total.astype(BF16).astype(wire)
        return carry

    lax.fori_loop(0, nb, g_long, 0, unroll=4)

    def g_share(k):
        return pltpu.make_async_remote_copy(
            src_ref=g2.at[mc], dst_ref=g2.at[mc],
            send_sem=gc_ss.at[k - 1], recv_sem=gc_rs.at[k - 1],
            device_id={"col": col_at(k)}, device_id_type=MESH,
        )

    def g_arrives(k):
        return pltpu.make_async_remote_copy(
            src_ref=g2.at[mc], dst_ref=g2.at[col_at(cols_n - k)],
            send_sem=gc_ss.at[k - 1], recv_sem=gc_rs.at[k - 1],
            device_id={"col": col_at(k)}, device_id_type=MESH,
        )

    g_shares = [g_share(k) for k in range(1, cols_n)]
    for copy in g_shares:
        copy.start()

    inner(z_band)
    zacc[0] = nt(xb[0], band_ref[0, 1]) + nt(xb[1], band_ref[0, 2])
    zacc[last] = nt(xb[last - 1], band_ref[last, 0]) + nt(xb[last], band_ref[last, 1])

    for copy in operands[7:]:
        copy.wait()
    win_t = win_ref[...].astype(F32).T.astype(BF16)
    out_f = jnp.zeros((wout_ref.shape[0], hidden), F32)
    for c in range(cols_n):
        out_f += (mc == c).astype(F32) * wout_ref[:, c * hidden:(c + 1) * hidden].astype(F32)
    out_t = out_f.astype(BF16)
    my_out = out_f.T.astype(BF16)
    first_ref[...] = jnp.zeros_like(first_ref)
    second_ref[...] = jnp.zeros_like(second_ref)

    for pos in NEAR_FIRST:
        x_copies[pos].wait_recv()
        for rank in range(2):
            contrib[rank] = nt(xr[pos, rank], long_ref[read[pos][rank][0]])
        if pos == BEFORE:
            zacc[0] += nt(xr[pos, 2], band_ref[0, 0])
        if pos == BEYOND:
            zacc[last] += nt(xr[pos, 2], band_ref[last, 2])

        def z_long(r, carry, pos=pos):
            total = zacc[r]
            for rank in range(2):
                s, row, live = read[pos][rank]
                total += (live * (row == r).astype(F32)) * contrib[rank]
            if pos == NEAR_FIRST[-1]:
                z[:, lanes(r)] = total.astype(BF16)
            else:
                zacc[r] = total
            return carry

        lax.fori_loop(0, nb, z_long, 0, unroll=4)

    tile = 4 * BLK
    tiles = nodes // tile

    def tile_at(t):
        return pl.ds(t * tile, tile)

    def p_share(k, t):
        return pltpu.make_async_remote_copy(
            src_ref=part_out.at[col_at(k), :, tile_at(t)], dst_ref=part_in.at[k - 1, :, tile_at(t)],
            send_sem=p_ss.at[k - 1, t], recv_sem=p_rs.at[k - 1, t],
            device_id={"col": col_at(k)}, device_id_type=MESH,
        )

    p_shares = []
    for t in range(tiles):
        v = nn(win_t, z[:, tile_at(t)])
        sig = 0.5 * jnp.tanh(0.5 * v) + 0.5
        h = (v * sig).astype(BF16)
        p = nn(out_t, h)
        for c in range(cols_n):
            part[c, :, tile_at(t)] = p[c * cc:(c + 1) * cc]
            part_out[c, :, tile_at(t)] = p[c * cc:(c + 1) * cc].astype(wire)
        for k in range(1, cols_n):
            p_shares.append(p_share(k, t))
            p_shares[-1].start()
        if t == 0:
            for k in range(1, cols_n):
                g_arrives(k).wait_recv()
        g = g2[:, :, tile_at(t)].reshape(cols_n * cc, tile).astype(BF16)
        second_ref[...] += nt(g, h)
        ds = (nn(my_out, g) * (sig * (1.0 + v * (1.0 - sig)))).astype(BF16)
        first_ref[...] += nt(z[:, tile_at(t)], ds)

    if reduce_here:
        fr = first_ref.shape[0] // rows_n
        sr = second_ref.shape[0] // rows_n
        for j in range(rows_n):
            mine = [first_ref[j * fr:(j + 1) * fr], second_ref[j * sr:(j + 1) * sr]]
            if red.shape[2] > fr + sr:
                mine.append(jnp.zeros((red.shape[2] - fr - sr, hidden), F32))
            red[j % 2, j // 2] = jnp.concatenate(mine, 0)
        core = lax.rem(me, 2)
        chip = lax.div(me, 2)
        chips = rows_n // 2

        def chip_at(by):
            return lax.rem(chip + by, chips)

        def to_partner(src, dst, i):
            return pltpu.make_async_remote_copy(
                src_ref=src, dst_ref=dst, send_sem=pair_ss.at[i], recv_sem=pair_rs.at[i],
                device_id={"row": me + 1 - 2 * core}, device_id_type=MESH,
            )

        def red_copy(k):
            return pltpu.make_async_remote_copy(
                src_ref=half.at[chip_at(k)], dst_ref=red_in.at[k - 1],
                send_sem=red_ss.at[k - 1], recv_sem=red_rs.at[k - 1],
                device_id={"row": 2 * chip_at(k) + core}, device_id_type=MESH,
            )

        def all_copy(k, slot):
            return pltpu.make_async_remote_copy(
                src_ref=summed.at[core, chip], dst_ref=summed.at[core, slot],
                send_sem=all_ss.at[k - 1], recv_sem=all_rs.at[k - 1],
                device_id={"row": 2 * chip_at(k) + core}, device_id_type=MESH,
            )

        pair_sum = to_partner(red.at[1 - core], pair_in, 0)
        pair_sum.start()
        pair_sum.wait_recv()
        for j in range(chips):
            half[j] = (red[core, j] + pair_in[j]).astype(half.dtype)
        red_copies = [red_copy(k) for k in range(1, chips)]
        for copy in red_copies:
            copy.start()

    for copy in p_shares:
        copy.wait_recv()

    def class_block(r, carry):
        total = part[mc, :, lanes(r)]
        for k in range(cols_n - 1):
            total += part_in[k, :, lanes(r)].astype(F32)
        cls[r] = total.astype(BF16).astype(wire)
        return carry

    lax.fori_loop(0, nb, class_block, 0, unroll=4)

    for pos in range(6):
        for rank in range(2):
            cs[pos, rank] = cls[served[pos][rank]]
    cs[BEFORE, 2] = cls[nb - 1]
    cs[BEYOND, 2] = cls[0]
    c_copies = [swap(cs, cr, c_ss, c_rs, pos, row_at(-d)) for pos, d in enumerate(DISTANCES)]
    for copy in c_copies:
        copy.start()

    def s_band(r):
        values = jnp.concatenate([cls[r - 1], cls[r], cls[r + 1]], 1).astype(BF16)
        blocks = jnp.concatenate([band_ref[r, 0], band_ref[r, 1], band_ref[r, 2]], 1)
        gacc[r] = nt(values, blocks)

    inner(s_band)
    gacc[0] = nt(cls[0].astype(BF16), band_ref[0, 1]) + nt(cls[1].astype(BF16), band_ref[0, 2])
    gacc[last] = nt(cls[last - 1].astype(BF16), band_ref[last, 0]) + nt(cls[last].astype(BF16), band_ref[last, 1])

    if reduce_here:
        for copy in red_copies:
            copy.wait_recv()
        total = red[core, chip] + pair_in[chip]
        for k in range(chips - 1):
            total += red_in[k].astype(F32)
        summed[core, chip] = total.astype(summed.dtype)
        all_copies = [all_copy(k, chip) for k in range(1, chips)]
        for copy in all_copies:
            copy.start()

    for copy in c_copies:
        copy.wait_recv()
    for pos in range(6):
        for rank in range(2):
            s, row, live = read[pos][rank]
            contrib[2 * pos + rank, 0:cc] = nt(cr[pos, rank].astype(BF16), long_ref[s])
    gacc[0] += nt(cr[BEFORE, 2].astype(BF16), band_ref[0, 0])
    gacc[nb - 1] += nt(cr[BEYOND, 2].astype(BF16), band_ref[nb - 1, 2])

    def s_long(r, carry):
        total = gacc[r]
        for pos in range(6):
            for rank in range(2):
                s, row, live = read[pos][rank]
                total += (live * (row == r).astype(F32)) * contrib[2 * pos + rank, 0:cc]
        scores_ref[:, lanes(r)] = total.astype(BF16)
        return carry

    lax.fori_loop(0, nb, s_long, 0, unroll=4)

    if reduce_here:
        for k in range(1, chips):
            all_copy(k, chip_at(chips - k)).wait_recv()
        pair_all = to_partner(summed.at[core], summed.at[core], 1)
        pair_all.start()
        to_partner(summed.at[1 - core], summed.at[1 - core], 1).wait_recv()
        for j in range(rows_n):
            final = summed[j % 2, j // 2].astype(F32)
            first_ref[j * fr:(j + 1) * fr] = final[0:fr]
            second_ref[j * sr:(j + 1) * sr] = final[fr:fr + sr]
        for copy in red_copies + all_copies + [pair_sum, pair_all]:
            copy.wait_send()

    for copy in x_copies + g_copies + c_copies + g_shares + p_shares:
        copy.wait_send()


def local(
    features, weight_in, weight_out, score_grad, band_blocks, long_blocks, long_rows, long_sources, long_counts,
):
    rows_n = lax.axis_size("row")
    cols_n = lax.axis_size("col")
    feats, nodes = features.shape
    nb = nodes // BLK
    hidden = weight_in.shape[1]
    cc = score_grad.shape[0]
    classes = weight_out.shape[1]
    wire = BF16 if cc % 16 == 0 else F32
    reduce_here = rows_n % 2 == 0 and feats % (8 * rows_n) == 0 and classes % rows_n == 0 and hidden % BLK == 0
    chunk = -(-((feats + classes) // rows_n) // 16) * 16 if reduce_here else 16
    chips = rows_n // 2 if reduce_here else 2
    peers = chips - 1
    dma = pltpu.SemaphoreType.DMA
    vmem = pl.BlockSpec(memory_space=pltpu.VMEM)
    scores, first, second = pl.pallas_call(
        functools.partial(kernel, rows_n, cols_n, reduce_here),
        out_shape=(
            jax.ShapeDtypeStruct((cc, nodes), BF16),
            jax.ShapeDtypeStruct((feats, hidden), F32),
            jax.ShapeDtypeStruct((classes, hidden), F32),
        ),
        in_specs=[pl.BlockSpec(memory_space=pltpu.HBM)] * 9,
        out_specs=(vmem, vmem, vmem),
        scratch_shapes=[
            pltpu.VMEM(features.shape, BF16),
            pltpu.VMEM(weight_in.shape, BF16),
            pltpu.VMEM(weight_out.shape[::-1], BF16),
            pltpu.VMEM(score_grad.shape, BF16),
            pltpu.VMEM(band_blocks.shape, BF16),
            pltpu.VMEM(long_blocks.shape, BF16),
            pltpu.SMEM(long_rows.shape, jnp.int32),
            pltpu.SMEM(long_sources.shape, jnp.int32),
            pltpu.SMEM(long_counts.shape, jnp.int32),
            dma((9,)),
            pltpu.VMEM((nb, feats, BLK), BF16),
            pltpu.VMEM((nb, cc, BLK), wire),
            pltpu.VMEM((6, 3, feats, BLK), BF16),
            pltpu.VMEM((6, 3, feats, BLK), BF16),
            pltpu.VMEM((6, 3, cc, BLK), wire),
            pltpu.VMEM((6, 3, cc, BLK), wire),
            pltpu.VMEM((6, 3, cc, BLK), wire),
            pltpu.VMEM((6, 3, cc, BLK), wire),
            pltpu.VMEM((nb, feats, BLK), F32),
            pltpu.VMEM((SLOTS, feats, BLK), F32),
            pltpu.VMEM((feats, nodes), BF16),
            pltpu.VMEM((nb, cc, BLK), F32),
            pltpu.VMEM((cols_n, cc, nodes), wire),
            pltpu.VMEM((cols_n, cc, nodes), F32),
            pltpu.VMEM((cols_n, cc, nodes), wire),
            pltpu.VMEM((cols_n - 1, cc, nodes), wire),
            pltpu.VMEM((nb, cc, BLK), wire),
            pltpu.VMEM((2, chips, chunk, hidden), F32),
            pltpu.VMEM((chips, chunk, hidden), F32),
            pltpu.VMEM((chips, chunk, hidden), BF16),
            pltpu.VMEM((peers, chunk, hidden), BF16),
            pltpu.VMEM((2, chips, chunk, hidden), BF16),
            dma((6,)), dma((6,)), dma((6,)), dma((6,)), dma((6,)), dma((6,)),
            dma((cols_n - 1,)), dma((cols_n - 1,)), dma((cols_n - 1, nodes // (4 * BLK))), dma((cols_n - 1, nodes // (4 * BLK))),
            dma((peers,)), dma((peers,)), dma((peers,)), dma((peers,)), dma((2,)), dma((2,)),
        ],
        compiler_params=pltpu.CompilerParams(
            collective_id=0, has_side_effects=True, vmem_limit_bytes=32 * 1024 * 1024
        ),
    )(features, weight_in, weight_out.T, score_grad, band_blocks, long_blocks, long_rows, long_sources, long_counts)
    second = second.T
    if not reduce_here:
        first, second = lax.psum((first, second), "row")
    return scores, first, second


def solution(mesh):
    return jax.shard_map(
        local,
        mesh=mesh,
        in_specs=(
            P(None, "row"),
            P(None, "col"),
            P(),
            P("col", "row"),
            P("row", None, None, None),
            P("row", None, None),
            P("row", None),
            P(),
            P(),
        ),
        out_specs=(P("col", "row"), P(None, "col"), P("col", None)),
        check_vma=False,
    )
```

```python
import functools

import jax
import jax.numpy as jnp
from jax import lax
from jax.experimental import pallas as pl
from jax.experimental.pallas import tpu as pltpu
from jax.sharding import PartitionSpec as P

BLK = 128
SLOTS = 12
VMEM_BYTES = 60 * 1024 * 1024
DISTANCES = (-3, -2, -1, 1, 2, 3)
BEFORE = DISTANCES.index(-1)
BEYOND = DISTANCES.index(1)
NEAR_FIRST = sorted(range(6), key=lambda pos: abs(DISTANCES[pos]))
MESH = pl.DeviceIdType.MESH
F32 = jnp.float32
BF16 = jnp.bfloat16


def nn(a, b):
    return lax.dot_general(a, b, (((1,), (0,)), ((), ())), preferred_element_type=F32)


def nt(a, b):
    return lax.dot_general(a, b, (((1,), (1,)), ((), ())), preferred_element_type=F32)


def lanes(block):
    if isinstance(block, int):
        return pl.ds(block * BLK, BLK)
    return pl.ds(pl.multiple_of(block * BLK, BLK), BLK)


def blocks_sent(pos):
    return 3 if pos in (BEFORE, BEYOND) else 2


def kernel(
    rows_n, cols_n, reduce_here,
    x_hbm, win_hbm, wout_hbm, sg_hbm, band_hbm, long_hbm, rows_hbm, src_hbm, count_hbm,
    scores_hbm, first_hbm, second_hbm,
    scores_ref, first_ref, second_ref, out_sem,
    x_ref, win_ref, wout_ref, sg_ref, band_ref, long_ref, rows_ref, src_ref, count_ref, in_sem,
    xb, sb, xs, xr, gs, gr, cs, cr, zacc, contrib, z, gacc, g2, part, part_out, part_in, cls, red, red_in, summed,
    x_ss, x_rs, g_ss, g_rs, c_ss, c_rs, gc_ss, gc_rs, p_ss, p_rs, red_ss, red_rs, all_ss, all_rs,
):
    me = lax.axis_index("row")
    mc = lax.axis_index("col")
    nodes = x_ref.shape[1]
    nb = nodes // BLK
    hidden = win_ref.shape[1]
    cc = sg_ref.shape[0]
    wire = gs.dtype

    operands = [
        pltpu.make_async_copy(src, dst, in_sem.at[i])
        for i, (src, dst) in enumerate((
            (rows_hbm, rows_ref), (src_hbm, src_ref), (count_hbm, count_ref), (sg_hbm, sg_ref), (long_hbm, long_ref),
            (x_hbm, x_ref), (band_hbm, band_ref), (win_hbm, win_ref), (wout_hbm, wout_ref),
        ))
    ]
    for copy in operands:
        copy.start()

    def row_at(by):
        return lax.rem(me + (by + rows_n), rows_n)

    def col_at(by):
        return lax.rem(mc + by, cols_n)

    barrier = pltpu.get_barrier_semaphore()
    if reduce_here:
        def greet(k, carry):
            pl.semaphore_signal(barrier, inc=1, device_id={"row": row_at(k)}, device_id_type=MESH)
            return carry
        lax.fori_loop(1, rows_n, greet, 0)
        expected = rows_n - 1
    else:
        for d in DISTANCES:
            pl.semaphore_signal(barrier, inc=1, device_id={"row": row_at(d)}, device_id_type=MESH)
        expected = len(DISTANCES)
    for k in range(1, cols_n):
        pl.semaphore_signal(barrier, inc=1, device_id={"col": col_at(k)}, device_id_type=MESH)
    expected += cols_n - 1

    def slots_of(owners, owner):
        low, high = jnp.int32(0), jnp.int32(0)
        for s in range(SLOTS):
            high = jnp.where(owners[s] == owner, s, high)
            low = jnp.where(owners[SLOTS - 1 - s] == owner, SLOTS - 1 - s, low)
        return low, high

    def owners_of(reader):
        return [lax.div(src_ref[reader, s], nb) for s in range(SLOTS)]

    for copy in operands[:3]:
        copy.wait()
    my_owners = owners_of(me)
    served, read = [], []
    for d in DISTANCES:
        reader = row_at(-d)
        served.append([
            jnp.clip(src_ref[reader, s] - me * nb, 0, nb - 1) for s in slots_of(owners_of(reader), me)
        ])
        read.append([
            (s, jnp.clip(rows_ref[0, s], 0, nb - 1), (s < count_ref[me]).astype(F32))
            for s in slots_of(my_owners, row_at(d))
        ])

    for copy in operands[3:5]:
        copy.wait()
    for r in range(nb):
        sb[r] = sg_ref[:, lanes(r)].astype(wire)
    for pos in range(6):
        for rank in range(2):
            s, row, live = read[pos][rank]
            gs[pos, rank] = (live * nn(sb[row].astype(BF16), long_ref[s])).astype(wire)
    for copy in operands[5:7]:
        copy.wait()
    gs[BEFORE, 2] = nn(sg_ref[:, lanes(0)], band_ref[0, 0]).astype(wire)
    gs[BEYOND, 2] = nn(sg_ref[:, lanes(nb - 1)], band_ref[nb - 1, 2]).astype(wire)
    for r in range(nb):
        xb[r] = x_ref[:, lanes(r)]
    for pos in range(6):
        for rank in range(2):
            xs[pos, rank] = xb[served[pos][rank]]
    xs[BEFORE, 2] = xb[nb - 1]
    xs[BEYOND, 2] = xb[0]

    pl.semaphore_wait(barrier, expected)

    def swap(src, dst, ss, rs, pos, to):
        span = pl.ds(0, blocks_sent(pos))
        return pltpu.make_async_remote_copy(
            src_ref=src.at[pos, span], dst_ref=dst.at[pos, span],
            send_sem=ss.at[pos], recv_sem=rs.at[pos],
            device_id={"row": to}, device_id_type=MESH,
        )

    g_copies = [swap(gs, gr, g_ss, g_rs, pos, row_at(d)) for pos, d in enumerate(DISTANCES)]
    x_copies = [swap(xs, xr, x_ss, x_rs, pos, row_at(-d)) for pos, d in enumerate(DISTANCES)]
    for copies in (g_copies, x_copies):
        for pos in reversed(NEAR_FIRST):
            copies[pos].start()

    def three(r):
        start = (r - 1) * BLK
        return pl.ds(start if isinstance(r, int) else pl.multiple_of(start, BLK), 3 * BLK)

    def inner(body):
        lax.fori_loop(1, nb - 1, lambda r, c: (body(r), c)[1], 0, unroll=7)

    def g_band(r):
        blocks = jnp.concatenate([band_ref[r - 1, 2], band_ref[r, 1], band_ref[r + 1, 0]], 0)
        gacc[r] = nn(sg_ref[:, three(r)], blocks)

    def z_band(r):
        blocks = jnp.concatenate([band_ref[r, 0], band_ref[r, 1], band_ref[r, 2]], 1)
        zacc[r] = nt(x_ref[:, three(r)], blocks)

    last = nb - 1
    inner(g_band)
    gacc[0] = nn(sg_ref[:, lanes(0)], band_ref[0, 1]) + nn(sg_ref[:, lanes(1)], band_ref[1, 0])
    gacc[last] = nn(sg_ref[:, lanes(last)], band_ref[last, 1]) + nn(sg_ref[:, lanes(last - 1)], band_ref[last - 1, 2])

    for copy in g_copies:
        copy.wait_recv()
    gacc[0] += gr[BEYOND, 2].astype(F32)
    gacc[nb - 1] += gr[BEFORE, 2].astype(F32)

    def g_long(r, carry):
        total = gacc[r]
        for pos in range(6):
            for rank in range(2):
                total += (served[pos][rank] == r).astype(F32) * gr[pos, rank].astype(F32)
        g2[mc, :, lanes(r)] = total.astype(BF16).astype(wire)
        return carry

    lax.fori_loop(0, nb, g_long, 0, unroll=4)

    def g_share(k):
        return pltpu.make_async_remote_copy(
            src_ref=g2.at[mc], dst_ref=g2.at[mc],
            send_sem=gc_ss.at[k - 1], recv_sem=gc_rs.at[k - 1],
            device_id={"col": col_at(k)}, device_id_type=MESH,
        )

    def g_arrives(k):
        return pltpu.make_async_remote_copy(
            src_ref=g2.at[mc], dst_ref=g2.at[col_at(cols_n - k)],
            send_sem=gc_ss.at[k - 1], recv_sem=gc_rs.at[k - 1],
            device_id={"col": col_at(k)}, device_id_type=MESH,
        )

    g_shares = [g_share(k) for k in range(1, cols_n)]
    for copy in g_shares:
        copy.start()

    inner(z_band)
    zacc[0] = nt(xb[0], band_ref[0, 1]) + nt(xb[1], band_ref[0, 2])
    zacc[last] = nt(xb[last - 1], band_ref[last, 0]) + nt(xb[last], band_ref[last, 1])

    for copy in operands[7:]:
        copy.wait()
    win_t = win_ref[...].astype(F32).T.astype(BF16)
    out_f = jnp.zeros((wout_ref.shape[0], hidden), F32)
    for c in range(cols_n):
        out_f += (mc == c).astype(F32) * wout_ref[:, c * hidden:(c + 1) * hidden].astype(F32)
    out_t = out_f.astype(BF16)
    my_out = out_f.T.astype(BF16)
    first_ref[...] = jnp.zeros_like(first_ref)
    second_ref[...] = jnp.zeros_like(second_ref)

    for pos in NEAR_FIRST:
        x_copies[pos].wait_recv()
        for rank in range(2):
            contrib[rank] = nt(xr[pos, rank], long_ref[read[pos][rank][0]])
        if pos == BEFORE:
            zacc[0] += nt(xr[pos, 2], band_ref[0, 0])
        if pos == BEYOND:
            zacc[last] += nt(xr[pos, 2], band_ref[last, 2])

        def z_long(r, carry, pos=pos):
            total = zacc[r]
            for rank in range(2):
                s, row, live = read[pos][rank]
                total += (live * (row == r).astype(F32)) * contrib[rank]
            if pos == NEAR_FIRST[-1]:
                z[:, lanes(r)] = total.astype(BF16)
            else:
                zacc[r] = total
            return carry

        lax.fori_loop(0, nb, z_long, 0, unroll=4)

    tile = 4 * BLK
    tiles = nodes // tile

    def tile_at(t):
        return pl.ds(t * tile, tile)

    def p_share(k, t):
        return pltpu.make_async_remote_copy(
            src_ref=part_out.at[col_at(k), :, tile_at(t)], dst_ref=part_in.at[k - 1, :, tile_at(t)],
            send_sem=p_ss.at[k - 1, t], recv_sem=p_rs.at[k - 1, t],
            device_id={"col": col_at(k)}, device_id_type=MESH,
        )

    p_shares = []
    for t in range(tiles):
        v = nn(win_t, z[:, tile_at(t)])
        sig = 0.5 * jnp.tanh(0.5 * v) + 0.5
        h = (v * sig).astype(BF16)
        p = nn(out_t, h)
        for c in range(cols_n):
            part[c, :, tile_at(t)] = p[c * cc:(c + 1) * cc]
            part_out[c, :, tile_at(t)] = p[c * cc:(c + 1) * cc].astype(wire)
        for k in range(1, cols_n):
            p_shares.append(p_share(k, t))
            p_shares[-1].start()
        if t == 0:
            for k in range(1, cols_n):
                g_arrives(k).wait_recv()
        g = g2[:, :, tile_at(t)].reshape(cols_n * cc, tile).astype(BF16)
        second_ref[...] += nt(g, h)
        ds = (nn(my_out, g) * (sig * (1.0 + v * (1.0 - sig)))).astype(BF16)
        first_ref[...] += nt(z[:, tile_at(t)], ds)

    if reduce_here:
        fr = first_ref.shape[0] // rows_n
        sr = second_ref.shape[0] // rows_n
        for j in range(rows_n):
            mine = [first_ref[j * fr:(j + 1) * fr], second_ref[j * sr:(j + 1) * sr]]
            if red.shape[1] > fr + sr:
                mine.append(jnp.zeros((red.shape[1] - fr - sr, hidden), F32))
            red[j] = jnp.concatenate(mine, 0).astype(red.dtype)

        def red_copy(k):
            return pltpu.make_async_remote_copy(
                src_ref=red.at[row_at(k)], dst_ref=red_in.at[k - 1],
                send_sem=red_ss.at[k - 1], recv_sem=red_rs.at[k - 1],
                device_id={"row": row_at(k)}, device_id_type=MESH,
            )

        def all_copy(k, slot):
            return pltpu.make_async_remote_copy(
                src_ref=summed.at[me], dst_ref=summed.at[slot],
                send_sem=all_ss.at[k - 1], recv_sem=all_rs.at[k - 1],
                device_id={"row": row_at(k)}, device_id_type=MESH,
            )

        def over_peers(body):
            lax.fori_loop(1, rows_n, lambda k, c: (body(k), c)[1], 0)

        over_peers(lambda k: red_copy(k).start())

    for copy in p_shares:
        copy.wait_recv()

    def class_block(r, carry):
        total = part[mc, :, lanes(r)]
        for k in range(cols_n - 1):
            total += part_in[k, :, lanes(r)].astype(F32)
        cls[r] = total.astype(BF16).astype(wire)
        return carry

    lax.fori_loop(0, nb, class_block, 0, unroll=4)

    for pos in range(6):
        for rank in range(2):
            cs[pos, rank] = cls[served[pos][rank]]
    cs[BEFORE, 2] = cls[nb - 1]
    cs[BEYOND, 2] = cls[0]
    c_copies = [swap(cs, cr, c_ss, c_rs, pos, row_at(-d)) for pos, d in enumerate(DISTANCES)]
    for copy in c_copies:
        copy.start()

    def s_band(r):
        values = jnp.concatenate([cls[r - 1], cls[r], cls[r + 1]], 1).astype(BF16)
        blocks = jnp.concatenate([band_ref[r, 0], band_ref[r, 1], band_ref[r, 2]], 1)
        gacc[r] = nt(values, blocks)

    inner(s_band)
    gacc[0] = nt(cls[0].astype(BF16), band_ref[0, 1]) + nt(cls[1].astype(BF16), band_ref[0, 2])
    gacc[last] = nt(cls[last - 1].astype(BF16), band_ref[last, 0]) + nt(cls[last].astype(BF16), band_ref[last, 1])

    if reduce_here:
        over_peers(lambda k: red_copy(k).wait_recv())
        total = red[me].astype(F32)
        for k in range(rows_n - 1):
            total += red_in[k].astype(F32)
        summed[me] = total.astype(summed.dtype)
        over_peers(lambda k: all_copy(k, me).start())

    for copy in c_copies:
        copy.wait_recv()
    for pos in range(6):
        for rank in range(2):
            s, row, live = read[pos][rank]
            contrib[2 * pos + rank, 0:cc] = nt(cr[pos, rank].astype(BF16), long_ref[s])
    gacc[0] += nt(cr[BEFORE, 2].astype(BF16), band_ref[0, 0])
    gacc[nb - 1] += nt(cr[BEYOND, 2].astype(BF16), band_ref[nb - 1, 2])

    def s_long(r, carry):
        total = gacc[r]
        for pos in range(6):
            for rank in range(2):
                s, row, live = read[pos][rank]
                total += (live * (row == r).astype(F32)) * contrib[2 * pos + rank, 0:cc]
        scores_ref[:, lanes(r)] = total.astype(BF16)
        return carry

    lax.fori_loop(0, nb, s_long, 0, unroll=4)

    results = [
        pltpu.make_async_copy(src, dst, out_sem.at[i])
        for i, (src, dst) in enumerate(((scores_ref, scores_hbm), (first_ref, first_hbm), (second_ref, second_hbm)))
    ]
    results[0].start()
    if reduce_here:
        over_peers(lambda k: all_copy(k, row_at(-k)).wait_recv())
        for j in range(rows_n):
            final = summed[j].astype(F32)
            first_ref[j * fr:(j + 1) * fr] = final[0:fr]
            second_ref[j * sr:(j + 1) * sr] = final[fr:fr + sr]
    results[1].start()
    results[2].start()
    if reduce_here:
        over_peers(lambda k: red_copy(k).wait_send())
        over_peers(lambda k: all_copy(k, me).wait_send())

    for copy in x_copies + g_copies + c_copies + g_shares + p_shares:
        copy.wait_send()
    for copy in results:
        copy.wait()


def hand_over(*refs):
    count = len(refs) // 2
    copies = [pltpu.make_async_copy(refs[i], refs[count + i], refs[-1].at[i]) for i in range(count)]
    for copy in copies:
        copy.start()
    for copy in copies:
        copy.wait()


def local(
    features, weight_in, weight_out, score_grad, band_blocks, long_blocks, long_rows, long_sources, long_counts,
):
    rows_n = lax.axis_size("row")
    cols_n = lax.axis_size("col")
    feats, nodes = features.shape
    nb = nodes // BLK
    hidden = weight_in.shape[1]
    cc = score_grad.shape[0]
    classes = weight_out.shape[1]
    wire = BF16 if cc % 16 == 0 else F32
    reduce_here = feats % (8 * rows_n) == 0 and classes % rows_n == 0 and hidden % BLK == 0
    chunk = -(-((feats + classes) // rows_n) // 16) * 16 if reduce_here else 16
    slices = rows_n if reduce_here else 1
    peers = max(slices - 1, 1)
    dma = pltpu.SemaphoreType.DMA
    hbm = pl.BlockSpec(memory_space=pl.ANY)
    scores, first, second = pl.pallas_call(
        functools.partial(kernel, rows_n, cols_n, reduce_here),
        out_shape=(
            jax.ShapeDtypeStruct((cc, nodes), BF16),
            jax.ShapeDtypeStruct((feats, hidden), F32),
            jax.ShapeDtypeStruct((classes, hidden), F32),
        ),
        in_specs=[hbm] * 9,
        out_specs=(hbm, hbm, hbm),
        scratch_shapes=[
            pltpu.VMEM((cc, nodes), BF16),
            pltpu.VMEM((feats, hidden), F32),
            pltpu.VMEM((classes, hidden), F32),
            dma((3,)),
            pltpu.VMEM(features.shape, BF16),
            pltpu.VMEM(weight_in.shape, BF16),
            pltpu.VMEM(weight_out.shape[::-1], BF16),
            pltpu.VMEM(score_grad.shape, BF16),
            pltpu.VMEM(band_blocks.shape, BF16),
            pltpu.VMEM(long_blocks.shape, BF16),
            pltpu.SMEM(long_rows.shape, jnp.int32),
            pltpu.SMEM(long_sources.shape, jnp.int32),
            pltpu.SMEM(long_counts.shape, jnp.int32),
            dma((9,)),
            pltpu.VMEM((nb, feats, BLK), BF16),
            pltpu.VMEM((nb, cc, BLK), wire),
            pltpu.VMEM((6, 3, feats, BLK), BF16),
            pltpu.VMEM((6, 3, feats, BLK), BF16),
            pltpu.VMEM((6, 3, cc, BLK), wire),
            pltpu.VMEM((6, 3, cc, BLK), wire),
            pltpu.VMEM((6, 3, cc, BLK), wire),
            pltpu.VMEM((6, 3, cc, BLK), wire),
            pltpu.VMEM((nb, feats, BLK), F32),
            pltpu.VMEM((SLOTS, feats, BLK), F32),
            pltpu.VMEM((feats, nodes), BF16),
            pltpu.VMEM((nb, cc, BLK), F32),
            pltpu.VMEM((cols_n, cc, nodes), wire),
            pltpu.VMEM((cols_n, cc, nodes), F32),
            pltpu.VMEM((cols_n, cc, nodes), wire),
            pltpu.VMEM((cols_n - 1, cc, nodes), wire),
            pltpu.VMEM((nb, cc, BLK), wire),
            pltpu.VMEM((slices, chunk, hidden), BF16),
            pltpu.VMEM((peers, chunk, hidden), BF16),
            pltpu.VMEM((slices, chunk, hidden), BF16),
            dma((6,)), dma((6,)), dma((6,)), dma((6,)), dma((6,)), dma((6,)),
            dma((cols_n - 1,)), dma((cols_n - 1,)), dma((cols_n - 1, nodes // (4 * BLK))), dma((cols_n - 1, nodes // (4 * BLK))),
            dma((peers,)), dma((peers,)), dma((peers,)), dma((peers,)),
        ],
        compiler_params=pltpu.CompilerParams(
            collective_id=0, has_side_effects=True, vmem_limit_bytes=VMEM_BYTES
        ),
    )(features, weight_in, weight_out.T, score_grad, band_blocks, long_blocks, long_rows, long_sources, long_counts)
    scores, first, second = pl.pallas_call(
        hand_over,
        out_shape=tuple(jax.ShapeDtypeStruct(a.shape, a.dtype) for a in (scores, first, second)),
        in_specs=[hbm] * 3,
        out_specs=(hbm, hbm, hbm),
        scratch_shapes=[dma((3,))],
        compiler_params=pltpu.CompilerParams(vmem_limit_bytes=VMEM_BYTES),
    )(scores, first, second)
    second = second.T
    if not reduce_here:
        first, second = lax.psum((first, second), "row")
    return scores, first, second


def solution(mesh):
    return jax.shard_map(
        local,
        mesh=mesh,
        in_specs=(
            P(None, "row"),
            P(None, "col"),
            P(),
            P("col", "row"),
            P("row", None, None, None),
            P("row", None, None),
            P("row", None),
            P(),
            P(),
        ),
        out_specs=(P("col", "row"), P(None, "col"), P("col", None)),
        check_vma=False,
    )
```

```python
import functools

import jax
import jax.numpy as jnp
from jax import lax
from jax.experimental import pallas as pl
from jax.experimental.pallas import tpu as pltpu
from jax.sharding import PartitionSpec as P

BLK = 128
SLOTS = 12
VMEM_BYTES = 60 * 1024 * 1024
DISTANCES = (-3, -2, -1, 1, 2, 3)
BEFORE = DISTANCES.index(-1)
BEYOND = DISTANCES.index(1)
NEAR_FIRST = sorted(range(6), key=lambda pos: abs(DISTANCES[pos]))
MESH = pl.DeviceIdType.MESH
F32 = jnp.float32
BF16 = jnp.bfloat16


def nn(a, b):
    return lax.dot_general(a, b, (((1,), (0,)), ((), ())), preferred_element_type=F32)


def nt(a, b):
    return lax.dot_general(a, b, (((1,), (1,)), ((), ())), preferred_element_type=F32)


def lanes(block):
    if isinstance(block, int):
        return pl.ds(block * BLK, BLK)
    return pl.ds(pl.multiple_of(block * BLK, BLK), BLK)


def blocks_sent(pos):
    return 3 if pos in (BEFORE, BEYOND) else 2


def kernel(
    rows_n, cols_n, reduce_here,
    x_hbm, win_hbm, wout_hbm, sg_hbm, band_hbm, long_hbm, rows_hbm, src_hbm, count_hbm,
    scores_hbm, first_hbm, second_hbm,
    scores_ref, first_ref, second_ref, out_sem,
    x_ref, win_ref, wout_ref, sg_ref, band_ref, long_ref, rows_ref, src_ref, count_ref, in_sem,
    xb, sb, xs, xr, gs, gr, cs, cr, zacc, contrib, z, gacc, g2, part, part_out, part_in, cls, red, red_in, summed,
    x_ss, x_rs, g_ss, g_rs, c_ss, c_rs, gc_ss, gc_rs, p_ss, p_rs, red_ss, red_rs, all_ss, all_rs,
):
    me = lax.axis_index("row")
    mc = lax.axis_index("col")
    nodes = x_ref.shape[1]
    nb = nodes // BLK
    hidden = win_ref.shape[1]
    cc = sg_ref.shape[0]
    wire = gs.dtype

    operands = [
        pltpu.make_async_copy(src, dst, in_sem.at[i])
        for i, (src, dst) in enumerate((
            (rows_hbm, rows_ref), (src_hbm, src_ref), (count_hbm, count_ref), (sg_hbm, sg_ref), (long_hbm, long_ref),
            (x_hbm, x_ref), (band_hbm, band_ref), (win_hbm, win_ref), (wout_hbm, wout_ref),
        ))
    ]
    for copy in operands:
        copy.start()

    def row_at(by):
        return lax.rem(me + (by + rows_n), rows_n)

    def col_at(by):
        return lax.rem(mc + by, cols_n)

    barrier = pltpu.get_barrier_semaphore()
    if reduce_here:
        def greet(k, carry):
            pl.semaphore_signal(barrier, inc=1, device_id={"row": row_at(k)}, device_id_type=MESH)
            return carry
        lax.fori_loop(1, rows_n, greet, 0, unroll=5)
        expected = rows_n - 1
    else:
        for d in DISTANCES:
            pl.semaphore_signal(barrier, inc=1, device_id={"row": row_at(d)}, device_id_type=MESH)
        expected = len(DISTANCES)
    for k in range(1, cols_n):
        pl.semaphore_signal(barrier, inc=1, device_id={"col": col_at(k)}, device_id_type=MESH)
    expected += cols_n - 1

    def slots_of(owners, owner):
        low, high = jnp.int32(0), jnp.int32(0)
        for s in range(SLOTS):
            high = jnp.where(owners[s] == owner, s, high)
            low = jnp.where(owners[SLOTS - 1 - s] == owner, SLOTS - 1 - s, low)
        return low, high

    def owners_of(reader):
        return [lax.div(src_ref[reader, s], nb) for s in range(SLOTS)]

    for copy in operands[:3]:
        copy.wait()
    my_owners = owners_of(me)
    served, read = [], []
    for d in DISTANCES:
        reader = row_at(-d)
        served.append([
            jnp.clip(src_ref[reader, s] - me * nb, 0, nb - 1) for s in slots_of(owners_of(reader), me)
        ])
        read.append([
            (s, jnp.clip(rows_ref[0, s], 0, nb - 1), (s < count_ref[me]).astype(F32))
            for s in slots_of(my_owners, row_at(d))
        ])

    for copy in operands[3:5]:
        copy.wait()
    for r in range(nb):
        sb[r] = sg_ref[:, lanes(r)].astype(wire)
    for pos in range(6):
        for rank in range(2):
            s, row, live = read[pos][rank]
            gs[pos, rank] = (live * nn(sb[row].astype(BF16), long_ref[s])).astype(wire)
    for copy in operands[5:7]:
        copy.wait()
    gs[BEFORE, 2] = nn(sg_ref[:, lanes(0)], band_ref[0, 0]).astype(wire)
    gs[BEYOND, 2] = nn(sg_ref[:, lanes(nb - 1)], band_ref[nb - 1, 2]).astype(wire)
    for r in range(nb):
        xb[r] = x_ref[:, lanes(r)]
    for pos in range(6):
        for rank in range(2):
            xs[pos, rank] = xb[served[pos][rank]]
    xs[BEFORE, 2] = xb[nb - 1]
    xs[BEYOND, 2] = xb[0]

    pl.semaphore_wait(barrier, expected)

    def swap(src, dst, ss, rs, pos, to):
        span = pl.ds(0, blocks_sent(pos))
        return pltpu.make_async_remote_copy(
            src_ref=src.at[pos, span], dst_ref=dst.at[pos, span],
            send_sem=ss.at[pos], recv_sem=rs.at[pos],
            device_id={"row": to}, device_id_type=MESH,
        )

    g_copies = [swap(gs, gr, g_ss, g_rs, pos, row_at(d)) for pos, d in enumerate(DISTANCES)]
    x_copies = [swap(xs, xr, x_ss, x_rs, pos, row_at(-d)) for pos, d in enumerate(DISTANCES)]
    for copies in (g_copies, x_copies):
        for pos in reversed(NEAR_FIRST):
            copies[pos].start()

    def three(r):
        start = (r - 1) * BLK
        return pl.ds(start if isinstance(r, int) else pl.multiple_of(start, BLK), 3 * BLK)

    def inner(body):
        lax.fori_loop(1, nb - 1, lambda r, c: (body(r), c)[1], 0, unroll=7)

    def g_band(r):
        blocks = jnp.concatenate([band_ref[r - 1, 2], band_ref[r, 1], band_ref[r + 1, 0]], 0)
        gacc[r] = nn(sg_ref[:, three(r)], blocks)

    def z_band(r):
        blocks = jnp.concatenate([band_ref[r, 0], band_ref[r, 1], band_ref[r, 2]], 1)
        zacc[r] = nt(x_ref[:, three(r)], blocks)

    last = nb - 1
    inner(g_band)
    gacc[0] = nn(sg_ref[:, lanes(0)], band_ref[0, 1]) + nn(sg_ref[:, lanes(1)], band_ref[1, 0])
    gacc[last] = nn(sg_ref[:, lanes(last)], band_ref[last, 1]) + nn(sg_ref[:, lanes(last - 1)], band_ref[last - 1, 2])

    for copy in g_copies:
        copy.wait_recv()
    gacc[0] += gr[BEYOND, 2].astype(F32)
    gacc[nb - 1] += gr[BEFORE, 2].astype(F32)

    def g_long(r, carry):
        total = gacc[r]
        for pos in range(6):
            for rank in range(2):
                total += (served[pos][rank] == r).astype(F32) * gr[pos, rank].astype(F32)
        g2[mc, :, lanes(r)] = total.astype(BF16).astype(wire)
        return carry

    lax.fori_loop(0, nb, g_long, 0, unroll=4)

    def g_share(k):
        return pltpu.make_async_remote_copy(
            src_ref=g2.at[mc], dst_ref=g2.at[mc],
            send_sem=gc_ss.at[k - 1], recv_sem=gc_rs.at[k - 1],
            device_id={"col": col_at(k)}, device_id_type=MESH,
        )

    def g_arrives(k):
        return pltpu.make_async_remote_copy(
            src_ref=g2.at[mc], dst_ref=g2.at[col_at(cols_n - k)],
            send_sem=gc_ss.at[k - 1], recv_sem=gc_rs.at[k - 1],
            device_id={"col": col_at(k)}, device_id_type=MESH,
        )

    g_shares = [g_share(k) for k in range(1, cols_n)]
    for copy in g_shares:
        copy.start()

    inner(z_band)
    zacc[0] = nt(xb[0], band_ref[0, 1]) + nt(xb[1], band_ref[0, 2])
    zacc[last] = nt(xb[last - 1], band_ref[last, 0]) + nt(xb[last], band_ref[last, 1])

    for copy in operands[7:]:
        copy.wait()
    win_t = win_ref[...].astype(F32).T.astype(BF16)
    out_f = jnp.zeros((wout_ref.shape[0], hidden), F32)
    for c in range(cols_n):
        out_f += (mc == c).astype(F32) * wout_ref[:, c * hidden:(c + 1) * hidden].astype(F32)
    out_t = out_f.astype(BF16)
    my_out = out_f.T.astype(BF16)
    first_ref[...] = jnp.zeros_like(first_ref)
    second_ref[...] = jnp.zeros_like(second_ref)

    for pos in NEAR_FIRST:
        x_copies[pos].wait_recv()
        for rank in range(2):
            contrib[rank] = nt(xr[pos, rank], long_ref[read[pos][rank][0]])
        if pos == BEFORE:
            zacc[0] += nt(xr[pos, 2], band_ref[0, 0])
        if pos == BEYOND:
            zacc[last] += nt(xr[pos, 2], band_ref[last, 2])

        def z_long(r, carry, pos=pos):
            total = zacc[r]
            for rank in range(2):
                s, row, live = read[pos][rank]
                total += (live * (row == r).astype(F32)) * contrib[rank]
            if pos == NEAR_FIRST[-1]:
                z[:, lanes(r)] = total.astype(BF16)
            else:
                zacc[r] = total
            return carry

        lax.fori_loop(0, nb, z_long, 0, unroll=4)

    tile = 4 * BLK
    tiles = nodes // tile

    def tile_at(t):
        return pl.ds(t * tile, tile)

    def p_share(k, t):
        return pltpu.make_async_remote_copy(
            src_ref=part_out.at[col_at(k), :, tile_at(t)], dst_ref=part_in.at[k - 1, :, tile_at(t)],
            send_sem=p_ss.at[k - 1, t], recv_sem=p_rs.at[k - 1, t],
            device_id={"col": col_at(k)}, device_id_type=MESH,
        )

    p_shares = []
    for t in range(tiles):
        v = nn(win_t, z[:, tile_at(t)])
        sig = 0.5 * jnp.tanh(0.5 * v) + 0.5
        h = (v * sig).astype(BF16)
        p = nn(out_t, h)
        for c in range(cols_n):
            part[c, :, tile_at(t)] = p[c * cc:(c + 1) * cc]
            part_out[c, :, tile_at(t)] = p[c * cc:(c + 1) * cc].astype(wire)
        for k in range(1, cols_n):
            p_shares.append(p_share(k, t))
            p_shares[-1].start()
        if t == 0:
            for k in range(1, cols_n):
                g_arrives(k).wait_recv()
        g = g2[:, :, tile_at(t)].reshape(cols_n * cc, tile).astype(BF16)
        second_ref[...] += nt(g, h)
        ds = (nn(my_out, g) * (sig * (1.0 + v * (1.0 - sig)))).astype(BF16)
        first_ref[...] += nt(z[:, tile_at(t)], ds)

    if reduce_here:
        fr = first_ref.shape[0] // rows_n
        sr = second_ref.shape[0] // rows_n
        for j in range(rows_n):
            mine = [first_ref[j * fr:(j + 1) * fr], second_ref[j * sr:(j + 1) * sr]]
            if red.shape[1] > fr + sr:
                mine.append(jnp.zeros((red.shape[1] - fr - sr, hidden), F32))
            red[j] = jnp.concatenate(mine, 0).astype(red.dtype)

        def red_copy(k):
            return pltpu.make_async_remote_copy(
                src_ref=red.at[row_at(k)], dst_ref=red_in.at[k - 1],
                send_sem=red_ss.at[k - 1], recv_sem=red_rs.at[k - 1],
                device_id={"row": row_at(k)}, device_id_type=MESH,
            )

        def all_copy(k, slot):
            return pltpu.make_async_remote_copy(
                src_ref=summed.at[me], dst_ref=summed.at[slot],
                send_sem=all_ss.at[k - 1], recv_sem=all_rs.at[k - 1],
                device_id={"row": row_at(k)}, device_id_type=MESH,
            )

        def over_peers(body):
            lax.fori_loop(1, rows_n, lambda k, c: (body(k), c)[1], 0, unroll=5)

        over_peers(lambda k: red_copy(k).start())

    for copy in p_shares:
        copy.wait_recv()

    def class_block(r, carry):
        total = part[mc, :, lanes(r)]
        for k in range(cols_n - 1):
            total += part_in[k, :, lanes(r)].astype(F32)
        cls[r] = total.astype(BF16).astype(wire)
        return carry

    lax.fori_loop(0, nb, class_block, 0, unroll=4)

    for pos in range(6):
        for rank in range(2):
            cs[pos, rank] = cls[served[pos][rank]]
    cs[BEFORE, 2] = cls[nb - 1]
    cs[BEYOND, 2] = cls[0]
    c_copies = [swap(cs, cr, c_ss, c_rs, pos, row_at(-d)) for pos, d in enumerate(DISTANCES)]
    for copy in c_copies:
        copy.start()

    def s_band(r):
        values = jnp.concatenate([cls[r - 1], cls[r], cls[r + 1]], 1).astype(BF16)
        blocks = jnp.concatenate([band_ref[r, 0], band_ref[r, 1], band_ref[r, 2]], 1)
        gacc[r] = nt(values, blocks)

    inner(s_band)
    gacc[0] = nt(cls[0].astype(BF16), band_ref[0, 1]) + nt(cls[1].astype(BF16), band_ref[0, 2])
    gacc[last] = nt(cls[last - 1].astype(BF16), band_ref[last, 0]) + nt(cls[last].astype(BF16), band_ref[last, 1])

    if reduce_here:
        over_peers(lambda k: red_copy(k).wait_recv())
        total = red[me].astype(F32)
        for k in range(rows_n - 1):
            total += red_in[k].astype(F32)
        summed[me] = total.astype(summed.dtype)
        over_peers(lambda k: all_copy(k, me).start())

    for copy in c_copies:
        copy.wait_recv()
    for pos in range(6):
        for rank in range(2):
            s, row, live = read[pos][rank]
            contrib[2 * pos + rank, 0:cc] = nt(cr[pos, rank].astype(BF16), long_ref[s])
    gacc[0] += nt(cr[BEFORE, 2].astype(BF16), band_ref[0, 0])
    gacc[nb - 1] += nt(cr[BEYOND, 2].astype(BF16), band_ref[nb - 1, 2])

    def s_long(r, carry):
        total = gacc[r]
        for pos in range(6):
            for rank in range(2):
                s, row, live = read[pos][rank]
                total += (live * (row == r).astype(F32)) * contrib[2 * pos + rank, 0:cc]
        scores_ref[:, lanes(r)] = total.astype(BF16)
        return carry

    lax.fori_loop(0, nb, s_long, 0, unroll=4)

    results = [
        pltpu.make_async_copy(src, dst, out_sem.at[i])
        for i, (src, dst) in enumerate(((scores_ref, scores_hbm), (first_ref, first_hbm), (second_ref, second_hbm)))
    ]
    results[0].start()
    if reduce_here:
        over_peers(lambda k: all_copy(k, row_at(-k)).wait_recv())
        for j in range(rows_n):
            final = summed[j].astype(F32)
            first_ref[j * fr:(j + 1) * fr] = final[0:fr]
            second_ref[j * sr:(j + 1) * sr] = final[fr:fr + sr]
    results[1].start()
    results[2].start()
    if reduce_here:
        over_peers(lambda k: red_copy(k).wait_send())
        over_peers(lambda k: all_copy(k, me).wait_send())

    for copy in x_copies + g_copies + c_copies + g_shares + p_shares:
        copy.wait_send()
    for copy in results:
        copy.wait()


def hand_over(a, b, c, a_out, b_out, c_out, a_held, b_held, c_held, sem_in, sem_out):
    held = (a_held, b_held, c_held)
    arriving = [pltpu.make_async_copy(src, dst, sem_in.at[i]) for i, (src, dst) in enumerate(zip((a, b, c), held))]
    leaving = [
        pltpu.make_async_copy(src, dst, sem_out.at[i]) for i, (src, dst) in enumerate(zip(held, (a_out, b_out, c_out)))
    ]
    for copy in arriving:
        copy.start()
    for before, after in zip(arriving, leaving):
        before.wait()
        after.start()
    for copy in leaving:
        copy.wait()


def local(
    features, weight_in, weight_out, score_grad, band_blocks, long_blocks, long_rows, long_sources, long_counts,
):
    rows_n = lax.axis_size("row")
    cols_n = lax.axis_size("col")
    feats, nodes = features.shape
    nb = nodes // BLK
    hidden = weight_in.shape[1]
    cc = score_grad.shape[0]
    classes = weight_out.shape[1]
    wire = BF16 if cc % 16 == 0 else F32
    reduce_here = feats % (8 * rows_n) == 0 and classes % rows_n == 0 and hidden % BLK == 0
    chunk = -(-((feats + classes) // rows_n) // 16) * 16 if reduce_here else 16
    slices = rows_n if reduce_here else 1
    peers = max(slices - 1, 1)
    dma = pltpu.SemaphoreType.DMA
    hbm = pl.BlockSpec(memory_space=pl.ANY)
    scores, first, second = pl.pallas_call(
        functools.partial(kernel, rows_n, cols_n, reduce_here),
        out_shape=(
            jax.ShapeDtypeStruct((cc, nodes), BF16),
            jax.ShapeDtypeStruct((feats, hidden), F32),
            jax.ShapeDtypeStruct((classes, hidden), F32),
        ),
        in_specs=[hbm] * 9,
        out_specs=(hbm, hbm, hbm),
        scratch_shapes=[
            pltpu.VMEM((cc, nodes), BF16),
            pltpu.VMEM((feats, hidden), F32),
            pltpu.VMEM((classes, hidden), F32),
            dma((3,)),
            pltpu.VMEM(features.shape, BF16),
            pltpu.VMEM(weight_in.shape, BF16),
            pltpu.VMEM(weight_out.shape[::-1], BF16),
            pltpu.VMEM(score_grad.shape, BF16),
            pltpu.VMEM(band_blocks.shape, BF16),
            pltpu.VMEM(long_blocks.shape, BF16),
            pltpu.SMEM(long_rows.shape, jnp.int32),
            pltpu.SMEM(long_sources.shape, jnp.int32),
            pltpu.SMEM(long_counts.shape, jnp.int32),
            dma((9,)),
            pltpu.VMEM((nb, feats, BLK), BF16),
            pltpu.VMEM((nb, cc, BLK), wire),
            pltpu.VMEM((6, 3, feats, BLK), BF16),
            pltpu.VMEM((6, 3, feats, BLK), BF16),
            pltpu.VMEM((6, 3, cc, BLK), wire),
            pltpu.VMEM((6, 3, cc, BLK), wire),
            pltpu.VMEM((6, 3, cc, BLK), wire),
            pltpu.VMEM((6, 3, cc, BLK), wire),
            pltpu.VMEM((nb, feats, BLK), F32),
            pltpu.VMEM((SLOTS, feats, BLK), F32),
            pltpu.VMEM((feats, nodes), BF16),
            pltpu.VMEM((nb, cc, BLK), F32),
            pltpu.VMEM((cols_n, cc, nodes), wire),
            pltpu.VMEM((cols_n, cc, nodes), F32),
            pltpu.VMEM((cols_n, cc, nodes), wire),
            pltpu.VMEM((cols_n - 1, cc, nodes), wire),
            pltpu.VMEM((nb, cc, BLK), wire),
            pltpu.VMEM((slices, chunk, hidden), BF16),
            pltpu.VMEM((peers, chunk, hidden), BF16),
            pltpu.VMEM((slices, chunk, hidden), BF16),
            dma((6,)), dma((6,)), dma((6,)), dma((6,)), dma((6,)), dma((6,)),
            dma((cols_n - 1,)), dma((cols_n - 1,)), dma((cols_n - 1, nodes // (4 * BLK))), dma((cols_n - 1, nodes // (4 * BLK))),
            dma((peers,)), dma((peers,)), dma((peers,)), dma((peers,)),
        ],
        compiler_params=pltpu.CompilerParams(
            collective_id=0, has_side_effects=True, vmem_limit_bytes=VMEM_BYTES
        ),
    )(features, weight_in, weight_out.T, score_grad, band_blocks, long_blocks, long_rows, long_sources, long_counts)
    scores, first, second = pl.pallas_call(
        hand_over,
        out_shape=tuple(jax.ShapeDtypeStruct(a.shape, a.dtype) for a in (scores, first, second)),
        in_specs=[hbm] * 3,
        out_specs=(hbm, hbm, hbm),
        scratch_shapes=[pltpu.VMEM(a.shape, a.dtype) for a in (scores, first, second)] + [dma((3,)), dma((3,))],
        compiler_params=pltpu.CompilerParams(vmem_limit_bytes=VMEM_BYTES),
    )(scores, first, second)
    second = second.T
    if not reduce_here:
        first, second = lax.psum((first, second), "row")
    return scores, first, second


def solution(mesh):
    return jax.shard_map(
        local,
        mesh=mesh,
        in_specs=(
            P(None, "row"),
            P(None, "col"),
            P(),
            P("col", "row"),
            P("row", None, None, None),
            P("row", None, None),
            P("row", None),
            P(),
            P(),
        ),
        out_specs=(P("col", "row"), P(None, "col"), P("col", None)),
        check_vma=False,
    )
```

```python
import functools

import jax
import jax.numpy as jnp
from jax import lax
from jax.experimental import pallas as pl
from jax.experimental.pallas import tpu as pltpu
from jax.sharding import PartitionSpec as P

BLK = 128
SLOTS = 12
VMEM_BYTES = 60 * 1024 * 1024
DISTANCES = (-3, -2, -1, 1, 2, 3)
BEFORE = DISTANCES.index(-1)
BEYOND = DISTANCES.index(1)
NEAR_FIRST = sorted(range(6), key=lambda pos: abs(DISTANCES[pos]))
MESH = pl.DeviceIdType.MESH
F32 = jnp.float32
BF16 = jnp.bfloat16


def nn(a, b):
    return lax.dot_general(a, b, (((1,), (0,)), ((), ())), preferred_element_type=F32)


def nt(a, b):
    return lax.dot_general(a, b, (((1,), (1,)), ((), ())), preferred_element_type=F32)


def lanes(block):
    if isinstance(block, int):
        return pl.ds(block * BLK, BLK)
    return pl.ds(pl.multiple_of(block * BLK, BLK), BLK)


def blocks_sent(pos):
    return 3 if pos in (BEFORE, BEYOND) else 2


def kernel(
    rows_n, cols_n, reduce_here,
    x_hbm, win_hbm, wout_hbm, sg_hbm, band_hbm, long_hbm, rows_hbm, src_hbm, count_hbm,
    scores_hbm, first_hbm, second_hbm,
    scores_ref, first_ref, second_ref, out_sem,
    x_ref, win_ref, wout_ref, sg_ref, band_ref, long_ref, rows_ref, src_ref, count_ref, in_sem,
    xb, sb, xs, xr, gs, gr, cs, cr, zacc, contrib, z, gacc, g2, act, slope, part, part_out, part_in, cls, red, red_in, summed,
    x_ss, x_rs, g_ss, g_rs, c_ss, c_rs, gc_ss, gc_rs, p_ss, p_rs, red_ss, red_rs, all_ss, all_rs,
):
    me = lax.axis_index("row")
    mc = lax.axis_index("col")
    nodes = x_ref.shape[1]
    nb = nodes // BLK
    hidden = win_ref.shape[1]
    cc = sg_ref.shape[0]
    wire = gs.dtype

    operands = [
        pltpu.make_async_copy(src, dst, in_sem.at[i])
        for i, (src, dst) in enumerate((
            (rows_hbm, rows_ref), (src_hbm, src_ref), (count_hbm, count_ref), (sg_hbm, sg_ref), (long_hbm, long_ref),
            (x_hbm, x_ref), (band_hbm, band_ref), (win_hbm, win_ref), (wout_hbm, wout_ref),
        ))
    ]
    for copy in operands:
        copy.start()

    def row_at(by):
        return lax.rem(me + (by + rows_n), rows_n)

    def col_at(by):
        return lax.rem(mc + by, cols_n)

    barrier = pltpu.get_barrier_semaphore()
    if reduce_here:
        def greet(k, carry):
            pl.semaphore_signal(barrier, inc=1, device_id={"row": row_at(k)}, device_id_type=MESH)
            return carry
        lax.fori_loop(1, rows_n, greet, 0, unroll=5)
        expected = rows_n - 1
    else:
        for d in DISTANCES:
            pl.semaphore_signal(barrier, inc=1, device_id={"row": row_at(d)}, device_id_type=MESH)
        expected = len(DISTANCES)
    for k in range(1, cols_n):
        pl.semaphore_signal(barrier, inc=1, device_id={"col": col_at(k)}, device_id_type=MESH)
    expected += cols_n - 1

    def slots_of(owners, owner):
        low, high = jnp.int32(0), jnp.int32(0)
        for s in range(SLOTS):
            high = jnp.where(owners[s] == owner, s, high)
            low = jnp.where(owners[SLOTS - 1 - s] == owner, SLOTS - 1 - s, low)
        return low, high

    def owners_of(reader):
        return [lax.div(src_ref[reader, s], nb) for s in range(SLOTS)]

    for copy in operands[:3]:
        copy.wait()
    my_owners = owners_of(me)
    served, read = [], []
    for d in DISTANCES:
        reader = row_at(-d)
        served.append([
            jnp.clip(src_ref[reader, s] - me * nb, 0, nb - 1) for s in slots_of(owners_of(reader), me)
        ])
        read.append([
            (s, jnp.clip(rows_ref[0, s], 0, nb - 1), (s < count_ref[me]).astype(F32))
            for s in slots_of(my_owners, row_at(d))
        ])

    operands[5].wait()
    for r in range(nb):
        xb[r] = x_ref[:, lanes(r)]
    for pos in range(6):
        for rank in range(2):
            xs[pos, rank] = xb[served[pos][rank]]
    xs[BEFORE, 2] = xb[nb - 1]
    xs[BEYOND, 2] = xb[0]

    pl.semaphore_wait(barrier, expected)

    def swap(src, dst, ss, rs, pos, to):
        span = pl.ds(0, blocks_sent(pos))
        return pltpu.make_async_remote_copy(
            src_ref=src.at[pos, span], dst_ref=dst.at[pos, span],
            send_sem=ss.at[pos], recv_sem=rs.at[pos],
            device_id={"row": to}, device_id_type=MESH,
        )

    g_copies = [swap(gs, gr, g_ss, g_rs, pos, row_at(d)) for pos, d in enumerate(DISTANCES)]
    x_copies = [swap(xs, xr, x_ss, x_rs, pos, row_at(-d)) for pos, d in enumerate(DISTANCES)]
    for pos in reversed(NEAR_FIRST):
        x_copies[pos].start()

    for copy in operands[3:5] + operands[6:7]:
        copy.wait()
    for r in range(nb):
        sb[r] = sg_ref[:, lanes(r)].astype(wire)
    for pos in range(6):
        for rank in range(2):
            s, row, live = read[pos][rank]
            gs[pos, rank] = (live * nn(sb[row].astype(BF16), long_ref[s])).astype(wire)
    gs[BEFORE, 2] = nn(sg_ref[:, lanes(0)], band_ref[0, 0]).astype(wire)
    gs[BEYOND, 2] = nn(sg_ref[:, lanes(nb - 1)], band_ref[nb - 1, 2]).astype(wire)
    for pos in reversed(NEAR_FIRST):
        g_copies[pos].start()

    def three(r):
        start = (r - 1) * BLK
        return pl.ds(start if isinstance(r, int) else pl.multiple_of(start, BLK), 3 * BLK)

    def inner(body):
        lax.fori_loop(1, nb - 1, lambda r, c: (body(r), c)[1], 0, unroll=7)

    def g_band(r):
        blocks = jnp.concatenate([band_ref[r - 1, 2], band_ref[r, 1], band_ref[r + 1, 0]], 0)
        gacc[r] = nn(sg_ref[:, three(r)], blocks)

    def z_band(r):
        blocks = jnp.concatenate([band_ref[r, 0], band_ref[r, 1], band_ref[r, 2]], 1)
        zacc[r] = nt(x_ref[:, three(r)], blocks)

    last = nb - 1
    inner(g_band)
    gacc[0] = nn(sg_ref[:, lanes(0)], band_ref[0, 1]) + nn(sg_ref[:, lanes(1)], band_ref[1, 0])
    gacc[last] = nn(sg_ref[:, lanes(last)], band_ref[last, 1]) + nn(sg_ref[:, lanes(last - 1)], band_ref[last - 1, 2])

    for copy in g_copies:
        copy.wait_recv()
    gacc[0] += gr[BEYOND, 2].astype(F32)
    gacc[nb - 1] += gr[BEFORE, 2].astype(F32)

    def g_long(r, carry):
        total = gacc[r]
        for pos in range(6):
            for rank in range(2):
                total += (served[pos][rank] == r).astype(F32) * gr[pos, rank].astype(F32)
        g2[mc, :, lanes(r)] = total.astype(BF16).astype(wire)
        return carry

    lax.fori_loop(0, nb, g_long, 0, unroll=4)

    def g_share(k):
        return pltpu.make_async_remote_copy(
            src_ref=g2.at[mc], dst_ref=g2.at[mc],
            send_sem=gc_ss.at[k - 1], recv_sem=gc_rs.at[k - 1],
            device_id={"col": col_at(k)}, device_id_type=MESH,
        )

    def g_arrives(k):
        return pltpu.make_async_remote_copy(
            src_ref=g2.at[mc], dst_ref=g2.at[col_at(cols_n - k)],
            send_sem=gc_ss.at[k - 1], recv_sem=gc_rs.at[k - 1],
            device_id={"col": col_at(k)}, device_id_type=MESH,
        )

    g_shares = [g_share(k) for k in range(1, cols_n)]
    for copy in g_shares:
        copy.start()

    inner(z_band)
    zacc[0] = nt(xb[0], band_ref[0, 1]) + nt(xb[1], band_ref[0, 2])
    zacc[last] = nt(xb[last - 1], band_ref[last, 0]) + nt(xb[last], band_ref[last, 1])

    for copy in operands[7:]:
        copy.wait()
    win_t = win_ref[...].astype(F32).T.astype(BF16)
    out_f = jnp.zeros((wout_ref.shape[0], hidden), F32)
    for c in range(cols_n):
        out_f += (mc == c).astype(F32) * wout_ref[:, c * hidden:(c + 1) * hidden].astype(F32)
    out_t = out_f.astype(BF16)
    my_out = out_f.T.astype(BF16)
    first_ref[...] = jnp.zeros_like(first_ref)
    second_ref[...] = jnp.zeros_like(second_ref)

    for pos in NEAR_FIRST:
        x_copies[pos].wait_recv()
        for rank in range(2):
            contrib[rank] = nt(xr[pos, rank], long_ref[read[pos][rank][0]])
        if pos == BEFORE:
            zacc[0] += nt(xr[pos, 2], band_ref[0, 0])
        if pos == BEYOND:
            zacc[last] += nt(xr[pos, 2], band_ref[last, 2])

        def z_long(r, carry, pos=pos):
            total = zacc[r]
            for rank in range(2):
                s, row, live = read[pos][rank]
                total += (live * (row == r).astype(F32)) * contrib[rank]
            if pos == NEAR_FIRST[-1]:
                z[:, lanes(r)] = total.astype(BF16)
            else:
                zacc[r] = total
            return carry

        lax.fori_loop(0, nb, z_long, 0, unroll=4)

    tile = 4 * BLK
    tiles = nodes // tile

    def tile_at(t):
        return pl.ds(t * tile, tile)

    def p_share(k, t):
        return pltpu.make_async_remote_copy(
            src_ref=part_out.at[col_at(k), :, tile_at(t)], dst_ref=part_in.at[k - 1, :, tile_at(t)],
            send_sem=p_ss.at[k - 1, t], recv_sem=p_rs.at[k - 1, t],
            device_id={"col": col_at(k)}, device_id_type=MESH,
        )

    p_shares = []
    for t in range(tiles):
        v = nn(win_t, z[:, tile_at(t)])
        sig = 0.5 * jnp.tanh(0.5 * v) + 0.5
        h = (v * sig).astype(BF16)
        p = nn(out_t, h)
        for c in range(cols_n):
            part[c, :, tile_at(t)] = p[c * cc:(c + 1) * cc]
            part_out[c, :, tile_at(t)] = p[c * cc:(c + 1) * cc].astype(wire)
        for k in range(1, cols_n):
            p_shares.append(p_share(k, t))
            p_shares[-1].start()
        act[:, tile_at(t)] = h
        slope[:, tile_at(t)] = sig * (1.0 + v * (1.0 - sig))

    for k in range(1, cols_n):
        g_arrives(k).wait_recv()
    for t in range(tiles):
        h = act[:, tile_at(t)]
        g = g2[:, :, tile_at(t)].reshape(cols_n * cc, tile).astype(BF16)
        second_ref[...] += nt(g, h)
        ds = (nn(my_out, g) * slope[:, tile_at(t)]).astype(BF16)
        first_ref[...] += nt(z[:, tile_at(t)], ds)

    if reduce_here:
        fr = first_ref.shape[0] // rows_n
        sr = second_ref.shape[0] // rows_n
        for j in range(rows_n):
            mine = [first_ref[j * fr:(j + 1) * fr], second_ref[j * sr:(j + 1) * sr]]
            if red.shape[1] > fr + sr:
                mine.append(jnp.zeros((red.shape[1] - fr - sr, hidden), F32))
            red[j] = jnp.concatenate(mine, 0).astype(red.dtype)

        def red_copy(k):
            return pltpu.make_async_remote_copy(
                src_ref=red.at[row_at(k)], dst_ref=red_in.at[k - 1],
                send_sem=red_ss.at[k - 1], recv_sem=red_rs.at[k - 1],
                device_id={"row": row_at(k)}, device_id_type=MESH,
            )

        def all_copy(k, slot):
            return pltpu.make_async_remote_copy(
                src_ref=summed.at[me], dst_ref=summed.at[slot],
                send_sem=all_ss.at[k - 1], recv_sem=all_rs.at[k - 1],
                device_id={"row": row_at(k)}, device_id_type=MESH,
            )

        def over_peers(body):
            lax.fori_loop(1, rows_n, lambda k, c: (body(k), c)[1], 0, unroll=5)

        over_peers(lambda k: red_copy(k).start())

    for copy in p_shares:
        copy.wait_recv()

    def class_block(r, carry):
        total = part[mc, :, lanes(r)]
        for k in range(cols_n - 1):
            total += part_in[k, :, lanes(r)].astype(F32)
        cls[r] = total.astype(BF16).astype(wire)
        return carry

    lax.fori_loop(0, nb, class_block, 0, unroll=4)

    for pos in range(6):
        for rank in range(2):
            cs[pos, rank] = cls[served[pos][rank]]
    cs[BEFORE, 2] = cls[nb - 1]
    cs[BEYOND, 2] = cls[0]
    c_copies = [swap(cs, cr, c_ss, c_rs, pos, row_at(-d)) for pos, d in enumerate(DISTANCES)]
    for copy in c_copies:
        copy.start()

    def s_band(r):
        values = jnp.concatenate([cls[r - 1], cls[r], cls[r + 1]], 1).astype(BF16)
        blocks = jnp.concatenate([band_ref[r, 0], band_ref[r, 1], band_ref[r, 2]], 1)
        gacc[r] = nt(values, blocks)

    inner(s_band)
    gacc[0] = nt(cls[0].astype(BF16), band_ref[0, 1]) + nt(cls[1].astype(BF16), band_ref[0, 2])
    gacc[last] = nt(cls[last - 1].astype(BF16), band_ref[last, 0]) + nt(cls[last].astype(BF16), band_ref[last, 1])

    if reduce_here:
        over_peers(lambda k: red_copy(k).wait_recv())
        total = red[me].astype(F32)
        for k in range(rows_n - 1):
            total += red_in[k].astype(F32)
        summed[me] = total.astype(summed.dtype)
        over_peers(lambda k: all_copy(k, me).start())

    for copy in c_copies:
        copy.wait_recv()
    for pos in range(6):
        for rank in range(2):
            s, row, live = read[pos][rank]
            contrib[2 * pos + rank, 0:cc] = nt(cr[pos, rank].astype(BF16), long_ref[s])
    gacc[0] += nt(cr[BEFORE, 2].astype(BF16), band_ref[0, 0])
    gacc[nb - 1] += nt(cr[BEYOND, 2].astype(BF16), band_ref[nb - 1, 2])

    def s_long(r, carry):
        total = gacc[r]
        for pos in range(6):
            for rank in range(2):
                s, row, live = read[pos][rank]
                total += (live * (row == r).astype(F32)) * contrib[2 * pos + rank, 0:cc]
        scores_ref[:, lanes(r)] = total.astype(BF16)
        return carry

    lax.fori_loop(0, nb, s_long, 0, unroll=4)

    results = [
        pltpu.make_async_copy(src, dst, out_sem.at[i])
        for i, (src, dst) in enumerate(((scores_ref, scores_hbm), (first_ref, first_hbm), (second_ref, second_hbm)))
    ]
    results[0].start()
    if reduce_here:
        over_peers(lambda k: all_copy(k, row_at(-k)).wait_recv())
        for j in range(rows_n):
            final = summed[j].astype(F32)
            first_ref[j * fr:(j + 1) * fr] = final[0:fr]
            second_ref[j * sr:(j + 1) * sr] = final[fr:fr + sr]
    results[1].start()
    results[2].start()
    if reduce_here:
        over_peers(lambda k: red_copy(k).wait_send())
        over_peers(lambda k: all_copy(k, me).wait_send())

    for copy in x_copies + g_copies + c_copies + g_shares + p_shares:
        copy.wait_send()
    for copy in results:
        copy.wait()


def hand_over(a, b, c, a_out, b_out, c_out, a_held, b_held, c_held, sem_in, sem_out):
    held = (a_held, b_held, c_held)
    arriving = [pltpu.make_async_copy(src, dst, sem_in.at[i]) for i, (src, dst) in enumerate(zip((a, b, c), held))]
    leaving = [
        pltpu.make_async_copy(src, dst, sem_out.at[i]) for i, (src, dst) in enumerate(zip(held, (a_out, b_out, c_out)))
    ]
    for copy in arriving:
        copy.start()
    for before, after in zip(arriving, leaving):
        before.wait()
        after.start()
    for copy in leaving:
        copy.wait()


def local(
    features, weight_in, weight_out, score_grad, band_blocks, long_blocks, long_rows, long_sources, long_counts,
):
    rows_n = lax.axis_size("row")
    cols_n = lax.axis_size("col")
    feats, nodes = features.shape
    nb = nodes // BLK
    hidden = weight_in.shape[1]
    cc = score_grad.shape[0]
    classes = weight_out.shape[1]
    wire = BF16 if cc % 16 == 0 else F32
    reduce_here = feats % (8 * rows_n) == 0 and classes % rows_n == 0 and hidden % BLK == 0
    chunk = -(-((feats + classes) // rows_n) // 16) * 16 if reduce_here else 16
    slices = rows_n if reduce_here else 1
    peers = max(slices - 1, 1)
    dma = pltpu.SemaphoreType.DMA
    hbm = pl.BlockSpec(memory_space=pl.ANY)
    scores, first, second = pl.pallas_call(
        functools.partial(kernel, rows_n, cols_n, reduce_here),
        out_shape=(
            jax.ShapeDtypeStruct((cc, nodes), BF16),
            jax.ShapeDtypeStruct((feats, hidden), F32),
            jax.ShapeDtypeStruct((classes, hidden), F32),
        ),
        in_specs=[hbm] * 9,
        out_specs=(hbm, hbm, hbm),
        scratch_shapes=[
            pltpu.VMEM((cc, nodes), BF16),
            pltpu.VMEM((feats, hidden), F32),
            pltpu.VMEM((classes, hidden), F32),
            dma((3,)),
            pltpu.VMEM(features.shape, BF16),
            pltpu.VMEM(weight_in.shape, BF16),
            pltpu.VMEM(weight_out.shape[::-1], BF16),
            pltpu.VMEM(score_grad.shape, BF16),
            pltpu.VMEM(band_blocks.shape, BF16),
            pltpu.VMEM(long_blocks.shape, BF16),
            pltpu.SMEM(long_rows.shape, jnp.int32),
            pltpu.SMEM(long_sources.shape, jnp.int32),
            pltpu.SMEM(long_counts.shape, jnp.int32),
            dma((9,)),
            pltpu.VMEM((nb, feats, BLK), BF16),
            pltpu.VMEM((nb, cc, BLK), wire),
            pltpu.VMEM((6, 3, feats, BLK), BF16),
            pltpu.VMEM((6, 3, feats, BLK), BF16),
            pltpu.VMEM((6, 3, cc, BLK), wire),
            pltpu.VMEM((6, 3, cc, BLK), wire),
            pltpu.VMEM((6, 3, cc, BLK), wire),
            pltpu.VMEM((6, 3, cc, BLK), wire),
            pltpu.VMEM((nb, feats, BLK), F32),
            pltpu.VMEM((SLOTS, feats, BLK), F32),
            pltpu.VMEM((feats, nodes), BF16),
            pltpu.VMEM((nb, cc, BLK), F32),
            pltpu.VMEM((cols_n, cc, nodes), wire),
            pltpu.VMEM((hidden, nodes), BF16),
            pltpu.VMEM((hidden, nodes), F32),
            pltpu.VMEM((cols_n, cc, nodes), F32),
            pltpu.VMEM((cols_n, cc, nodes), wire),
            pltpu.VMEM((cols_n - 1, cc, nodes), wire),
            pltpu.VMEM((nb, cc, BLK), wire),
            pltpu.VMEM((slices, chunk, hidden), BF16),
            pltpu.VMEM((peers, chunk, hidden), BF16),
            pltpu.VMEM((slices, chunk, hidden), BF16),
            dma((6,)), dma((6,)), dma((6,)), dma((6,)), dma((6,)), dma((6,)),
            dma((cols_n - 1,)), dma((cols_n - 1,)), dma((cols_n - 1, nodes // (4 * BLK))), dma((cols_n - 1, nodes // (4 * BLK))),
            dma((peers,)), dma((peers,)), dma((peers,)), dma((peers,)),
        ],
        compiler_params=pltpu.CompilerParams(
            collective_id=0, has_side_effects=True, vmem_limit_bytes=VMEM_BYTES
        ),
    )(features, weight_in, weight_out.T, score_grad, band_blocks, long_blocks, long_rows, long_sources, long_counts)
    scores, first, second = pl.pallas_call(
        hand_over,
        out_shape=tuple(jax.ShapeDtypeStruct(a.shape, a.dtype) for a in (scores, first, second)),
        in_specs=[hbm] * 3,
        out_specs=(hbm, hbm, hbm),
        scratch_shapes=[pltpu.VMEM(a.shape, a.dtype) for a in (scores, first, second)] + [dma((3,)), dma((3,))],
        compiler_params=pltpu.CompilerParams(vmem_limit_bytes=VMEM_BYTES),
    )(scores, first, second)
    second = second.T
    if not reduce_here:
        first, second = lax.psum((first, second), "row")
    return scores, first, second


def solution(mesh):
    return jax.shard_map(
        local,
        mesh=mesh,
        in_specs=(
            P(None, "row"),
            P(None, "col"),
            P(),
            P("col", "row"),
            P("row", None, None, None),
            P("row", None, None),
            P("row", None),
            P(),
            P(),
        ),
        out_specs=(P("col", "row"), P(None, "col"), P("col", None)),
        check_vma=False,
    )
```
